32 devices in a mesh: req: 8 (over y, x, core), mdl: 4 (over z).
Axes of the slice: x: 2, y: 2, z: 4, core: 2. Of those that a mesh axis runs over, the one named last changes fastest.
Arguments:
- hidden_in: bfloat16 [64, 16, 2048], P('req'), may hold values from -6 to 6
- mixer_gain: bfloat16 [2048], replicated, may hold values from 0.5 to 1.5
- w_query: bfloat16 [2048, 1024], P(None, 'mdl'), may hold values from -0.125 to 0.125
- w_kv: bfloat16 [2, 2048, 256], replicated, may hold values from -0.125 to 0.125
- w_attn_out: bfloat16 [1024, 2048], P('mdl'), may hold values from -0.1875 to 0.1875
- prompt_kv: bfloat16 [16, 2, 1024, 256], P('req')
- prompt_lengths: int32 [16], P('req'), may hold values from 1 to 1024, as said below
- member: int32 [64], P('req'), may hold values from 0 to 1
- accepted: int32 [64], P('req'), may hold values from 1 to 16, as said below
- w_z: bfloat16 [2048, 1536], P(None, 'mdl'), may hold values from -0.125 to 0.125
- w_x: bfloat16 [2048, 1536], P(None, 'mdl'), may hold values from -0.125 to 0.125
- w_bc: bfloat16 [2048, 512], replicated, may hold values from -0.125 to 0.125
- w_dt: bfloat16 [2048, 24], P(None, 'mdl'), may hold values from -0.125 to 0.125
- conv_x: bfloat16 [4, 1536], P(None, 'mdl'), may hold values from -1.5 to 1.5
- conv_bc: bfloat16 [4, 512], replicated, may hold values from -1.5 to 1.5
- ssm_rate: float32 [24], P('mdl'), may hold values from 1 to 16
- dt_bias: float32 [24], P('mdl'), may hold values from -4 to 0.5
- skip_d: float32 [24], P('mdl'), may hold values from 0.5 to 1.5
- prompt_state: float32 [16, 24, 64, 256], P('req', 'mdl'), may hold values from -0.4 to 0.4
- prompt_conv_x: bfloat16 [16, 3, 1536], P('req', None, 'mdl'), may hold values from -6 to 6
- prompt_conv_bc: bfloat16 [16, 3, 512], P('req'), may hold values from -6 to 6
- w_mamba_out: bfloat16 [1536, 2048], P('mdl'), may hold values from -0.15625 to 0.15625
- mlp_gain: bfloat16 [2048], replicated, may hold values from 0.5 to 1.5
- w_gate: bfloat16 [2048, 4096], P(None, 'req'), may hold values from -0.125 to 0.125
- w_up: bfloat16 [2048, 4096], P(None, 'req'), may hold values from -0.125 to 0.125
- w_down: bfloat16 [4096, 2048], P('req'), may hold values from -0.09375 to 0.09375
- final_gain: bfloat16 [2048], replicated, may hold values from 0.5 to 1.5
- head_weight: bfloat16 [32768, 2048], P('req')
- draft_ids: int32 [64, 16], replicated, may hold values from 0 to 32767
Outputs:
- hidden_out: bfloat16 [64, 16, 2048], P(('req', 'mdl'))
- verify_scores: float32 [64, 16], P(('req', 'mdl'))
- kept_state: float32 [64, 24, 64, 256], P(('req', 'mdl'))
- kept_conv: bfloat16 [64, 3, 2048], P(('req', 'mdl'))
The draws below stay inside these ranges and needn't reach their ends.
Inputs may be any that keep to these rules, and one draw needn't show every extreme that they name: Each request has accepted 1 to 16 drafts; both ends occur in every draw. `prompt_lengths`: a prompt of 1024 tokens occurs in every draw. `member`: index of the request's prompt among the 2 prompts of its block of 8 requests.
All inputs are finite; a program needn't handle non-finite values.
Results may differ from the reference program's by a relative error of at most 0.017.
Values may be sent and summed in bfloat16 or wider, within the bound.
A program may use at most 128 MiB of HBM per device.

```python
import math
import jax
import jax.numpy as jnp
from jax import lax

D = 2048
FF = 4096
VOCAB = 32768
Q_HEADS = 8
KV_HEADS = 2
HEAD_DIM = 128
SSM_HEADS = 24
SSM_DIM = 64
STATE = 256
CONV = 4
DRAFT = 16
PROMPTS = 2
P_MAX = 1024
ROW_REQ = 8
REQS = 64
NPROMPT = 16
TOKENS = 1024
SSM_INNER = 1536
N_REQ = 8


def draw_prompt_kv(key, part):
    values = jax.random.normal(key, (NPROMPT, KV_HEADS, P_MAX, 2 * HEAD_DIM), jnp.float32)
    return values.astype(jnp.bfloat16)


def draw_head_weight(key, part):
    values = jax.random.normal(key, (VOCAB, D), jnp.float32) * (3.0 / math.sqrt(D))
    return values.astype(jnp.bfloat16)


def draw_accepted(key, part):
    values = jax.random.randint(key, (REQS,), 1, DRAFT + 1)
    return values.at[0].set(DRAFT).at[1].set(1).astype(jnp.int32)


def draw_prompt_lengths(key, part):
    values = jax.random.randint(key, (NPROMPT,), 1, P_MAX + 1)
    return values.at[0].set(P_MAX).astype(jnp.int32)


def with_ends(array, key, least, top_value):
    longest = array.shape.index(max(array.shape))
    spots = []
    for shift in (0, 1):
        where = [jax.random.randint(jax.random.fold_in(key, axis), (), 0, length) for axis, length in enumerate(array.shape)]
        where[longest] = (where[longest] + shift) % array.shape[longest]
        spots.append(tuple(where))
    return array.at[spots[0]].set(least).at[spots[1]].set(top_value)


def steps_of(key, shape, shards, low, largest):
    level = 1.0
    for axis_at, blocks in shards:
        draws = jax.random.uniform(jax.random.fold_in(jax.random.fold_in(key, 6), axis_at), (blocks,), jnp.float32, low / len(shards), largest / len(shards))
        level = level * jnp.repeat(jnp.exp(draws), shape[axis_at] // blocks).reshape((-1,) + (1,) * (len(shape) - 1 - axis_at))
    return level


def scatter_about(rng, shape, scale, reach, split=(), held_as=jnp.bfloat16):
    entries = scale * jax.random.normal(rng, shape, jnp.float32)
    if split:
        entries = entries * steps_of(rng, shape, split, -0.22, 0.18)
    return jnp.clip(entries, -reach, reach).astype(held_as)


def setup_inputs(seed: int = 0) -> dict:
    streams_of = jax.random.split(jax.random.key(seed), 30)
    hidden_in = scatter_about(streams_of[0], (REQS, DRAFT, D), 1.0, 6.0, ((0, 8),))
    mixer_gain = jnp.clip(1.0 + 0.1 * jax.random.normal(streams_of[1], (D,), jnp.float32), 0.5, 1.5).astype(jnp.bfloat16)
    w_query = scatter_about(streams_of[2], (D, Q_HEADS * HEAD_DIM), D ** -0.5, 0.125, ((1, 4),))
    w_kv = scatter_about(streams_of[3], (KV_HEADS, D, 2 * HEAD_DIM), D ** -0.5, 0.125)
    w_attn_out = scatter_about(streams_of[4], (Q_HEADS * HEAD_DIM, D), (Q_HEADS * HEAD_DIM) ** -0.5, 0.1875, ((0, 4),))
    prompt_kv = draw_prompt_kv(jax.random.fold_in(streams_of[29], 71), 0)
    prompt_lengths = draw_prompt_lengths(jax.random.fold_in(streams_of[29], 71), 0)
    member = with_ends(jax.random.randint(streams_of[7], (REQS,), 0, PROMPTS), jax.random.fold_in(streams_of[7], 1), 0, PROMPTS - 1).astype(jnp.int32)
    accepted = draw_accepted(jax.random.fold_in(streams_of[29], 71), 0)
    w_z = scatter_about(streams_of[9], (D, SSM_INNER), D ** -0.5, 0.125, ((1, 4),))
    w_x = scatter_about(streams_of[10], (D, SSM_INNER), D ** -0.5, 0.125, ((1, 4),))
    w_bc = scatter_about(streams_of[11], (D, 2 * STATE), D ** -0.5, 0.125)
    w_dt = scatter_about(streams_of[12], (D, SSM_HEADS), D ** -0.5, 0.125, ((1, 4),))
    conv_x = scatter_about(streams_of[13], (CONV, SSM_INNER), 0.25, 1.5, ((1, 4),))
    conv_bc = scatter_about(streams_of[14], (CONV, 2 * STATE), 0.25, 1.5)
    ssm_rate = jnp.clip(jnp.exp(math.log(16.0) - 2.7725887 * jax.random.uniform(streams_of[15], (SSM_HEADS,), jnp.float32) ** steps_of(streams_of[15], (SSM_HEADS,), ((0, 4),), -0.2, 0.2)), 1.0, 16.0)
    dt_bias = jnp.clip(-4.0 + 4.5 * jax.random.uniform(streams_of[16], (SSM_HEADS,), jnp.float32) ** steps_of(streams_of[16], (SSM_HEADS,), ((0, 4),), -0.2, 0.2), -4.0, 0.5)
    skip_d = jnp.clip(0.5 + 1.0 * jax.random.uniform(streams_of[17], (SSM_HEADS,), jnp.float32) ** steps_of(streams_of[17], (SSM_HEADS,), ((0, 4),), -0.2, 0.2), 0.5, 1.5)
    prompt_state = scatter_about(streams_of[18], (NPROMPT, SSM_HEADS, SSM_DIM, STATE), 0.05, 0.4, ((0, 8), (1, 4)), jnp.float32)
    prompt_conv_x = scatter_about(streams_of[19], (NPROMPT, CONV - 1, SSM_INNER), 1.0, 6.0, ((0, 8), (2, 4)))
    prompt_conv_bc = scatter_about(streams_of[20], (NPROMPT, CONV - 1, 2 * STATE), 1.0, 6.0, ((0, 8),))
    w_mamba_out = scatter_about(streams_of[21], (SSM_INNER, D), SSM_INNER ** -0.5, 0.15625, ((0, 4),))
    mlp_gain = jnp.clip(1.0 + 0.1 * jax.random.normal(streams_of[22], (D,), jnp.float32), 0.5, 1.5).astype(jnp.bfloat16)
    w_gate = scatter_about(streams_of[23], (D, FF), D ** -0.5, 0.125, ((1, 8),))
    w_up = scatter_about(streams_of[24], (D, FF), D ** -0.5, 0.125, ((1, 8),))
    w_down = scatter_about(streams_of[25], (FF, D), FF ** -0.5, 0.09375, ((0, 8),))
    final_gain = jnp.clip(1.0 + 0.1 * jax.random.normal(streams_of[26], (D,), jnp.float32), 0.5, 1.5).astype(jnp.bfloat16)
    head_weight = draw_head_weight(jax.random.fold_in(streams_of[29], 71), 0)
    draft_ids = with_ends(jax.random.randint(streams_of[28], (REQS, DRAFT), 0, VOCAB), jax.random.fold_in(streams_of[28], 1), 0, VOCAB - 1).astype(jnp.int32)
    return dict(hidden_in=hidden_in, mixer_gain=mixer_gain, w_query=w_query, w_kv=w_kv, w_attn_out=w_attn_out, prompt_kv=prompt_kv, prompt_lengths=prompt_lengths, member=member, accepted=accepted, w_z=w_z, w_x=w_x, w_bc=w_bc, w_dt=w_dt, conv_x=conv_x, conv_bc=conv_bc, ssm_rate=ssm_rate, dt_bias=dt_bias, skip_d=skip_d, prompt_state=prompt_state, prompt_conv_x=prompt_conv_x, prompt_conv_bc=prompt_conv_bc, w_mamba_out=w_mamba_out, mlp_gain=mlp_gain, w_gate=w_gate, w_up=w_up, w_down=w_down, final_gain=final_gain, head_weight=head_weight, draft_ids=draft_ids)


eps_norm = 1e-05
far_below = -1e+30

def rms_scale(values, gain):
    widened = values.astype(jnp.float32)
    spread = lax.optimization_barrier(jnp.mean(widened * widened, axis=-1, keepdims=True))
    return widened * lax.rsqrt(spread + eps_norm) * gain.astype(jnp.float32)

def convolve(series, kernel, length):
    summed = jnp.zeros(series.shape[:-2] + (length, series.shape[-1]), jnp.float32)
    for kernel_tap in range(kernel.shape[0]):
        window = lax.slice_in_dim(series, kernel_tap, kernel_tap + length, axis=series.ndim - 2)
        summed = summed + window * kernel[kernel_tap].astype(jnp.float32)
    return jax.nn.silu(summed)

def reference(hidden_in, mixer_gain, w_query, w_kv, w_attn_out, prompt_kv, prompt_lengths, member, accepted, w_z, w_x, w_bc, w_dt, conv_x, conv_bc, ssm_rate, dt_bias, skip_d, prompt_state, prompt_conv_x, prompt_conv_bc, w_mamba_out, mlp_gain, w_gate, w_up, w_down, final_gain, head_weight, draft_ids):
    flat_rows = hidden_in.reshape(TOKENS, D)
    normed = rms_scale(flat_rows, mixer_gain).astype(jnp.bfloat16)
    queries = jnp.dot(normed, w_query, preferred_element_type=jnp.float32).astype(jnp.bfloat16)
    queries = queries.reshape(REQS, DRAFT, Q_HEADS, HEAD_DIM)
    key_value = jnp.stack([jnp.dot(normed, w_kv[group_index], preferred_element_type=jnp.float32) for group_index in range(KV_HEADS)], axis=1).astype(jnp.bfloat16)
    key_value = key_value.reshape(REQS, DRAFT, KV_HEADS, 2 * HEAD_DIM)
    slots = (jnp.arange(REQS) // ROW_REQ * PROMPTS + member).astype(jnp.int32)
    gate_z = jnp.dot(normed, w_z, preferred_element_type=jnp.float32).astype(jnp.bfloat16).reshape(REQS, DRAFT, SSM_INNER)
    ssm_in = jnp.dot(normed, w_x, preferred_element_type=jnp.float32).astype(jnp.bfloat16).reshape(REQS, DRAFT, SSM_INNER)
    bc_in = jnp.dot(normed, w_bc, preferred_element_type=jnp.float32).astype(jnp.bfloat16).reshape(REQS, DRAFT, 2 * STATE)
    dt_in = jnp.dot(normed, w_dt, preferred_element_type=jnp.float32).astype(jnp.bfloat16).reshape(REQS, DRAFT, SSM_HEADS)
    per_group = Q_HEADS // KV_HEADS
    score_scale = HEAD_DIM ** (-0.5)
    causal_pairs = jnp.arange(DRAFT)[None, :] <= jnp.arange(DRAFT)[:, None]

    def one_request(inputs):
        query_r, kv_r, prompt_slot, accepted_r, gate_r, input_r, bc_r, dt_r = inputs
        prompt_slot = prompt_slot.astype(jnp.int32)
        accepted_r = accepted_r.astype(jnp.int32)
        cached = lax.dynamic_index_in_dim(prompt_kv, prompt_slot, 0, keepdims=False)
        length = lax.dynamic_index_in_dim(prompt_lengths, prompt_slot, 0, keepdims=False)
        cached_heads = jnp.repeat(cached, per_group, axis=0).astype(jnp.float32)
        draft_heads = jnp.repeat(kv_r, per_group, axis=1).astype(jnp.float32)
        query_wide = query_r.astype(jnp.float32)
        prompt_scores = jnp.einsum('thd,hkd->htk', query_wide, cached_heads[:, :, :HEAD_DIM]) * score_scale
        prompt_valid = (jnp.arange(P_MAX) < length)[None, None, :]
        draft_scores = jnp.einsum('thd,shd->hts', query_wide, draft_heads[:, :, :HEAD_DIM]) * score_scale
        draft_valid = causal_pairs[None]
        row_top = jnp.maximum(lax.optimization_barrier(jnp.max(jnp.where(prompt_valid, prompt_scores, far_below), axis=-1)), lax.optimization_barrier(jnp.max(jnp.where(draft_valid, draft_scores, far_below), axis=-1)))
        prompt_weights = jnp.exp(jnp.where(prompt_valid, prompt_scores - row_top[..., None], far_below))
        draft_weights = jnp.exp(jnp.where(draft_valid, draft_scores - row_top[..., None], far_below))
        weight_total = lax.optimization_barrier(jnp.sum(prompt_weights, axis=-1)) + lax.optimization_barrier(jnp.sum(draft_weights, axis=-1))
        rounded_prompt = lax.optimization_barrier(prompt_weights.astype(jnp.bfloat16)).astype(jnp.float32)
        rounded_draft = lax.optimization_barrier(draft_weights.astype(jnp.bfloat16)).astype(jnp.float32)
        weighted = jnp.einsum('htk,hke->hte', rounded_prompt, cached_heads[:, :, HEAD_DIM:])
        weighted = weighted + jnp.einsum('hts,she->hte', rounded_draft, draft_heads[:, :, HEAD_DIM:])
        attended = (weighted / weight_total[..., None]).astype(jnp.bfloat16)
        attended = attended.transpose(1, 0, 2).reshape(DRAFT, Q_HEADS * HEAD_DIM)
        start_x = lax.dynamic_index_in_dim(prompt_conv_x, prompt_slot, 0, keepdims=False).astype(jnp.float32)
        start_bc = lax.dynamic_index_in_dim(prompt_conv_bc, prompt_slot, 0, keepdims=False).astype(jnp.float32)
        series_x = jnp.concatenate([start_x, input_r.astype(jnp.float32)], axis=0)
        series_bc = jnp.concatenate([start_bc, bc_r.astype(jnp.float32)], axis=0)
        conv_xs = convolve(series_x, conv_x, DRAFT)
        conv_bcs = convolve(series_bc, conv_bc, DRAFT)
        b_part = conv_bcs[:, :STATE]
        c_part = conv_bcs[:, STATE:]
        step_size = jax.nn.softplus(dt_r.astype(jnp.float32) + dt_bias)
        decay = jnp.exp(-step_size * ssm_rate)
        heads_x = conv_xs.reshape(DRAFT, SSM_HEADS, SSM_DIM)
        initial = lax.dynamic_index_in_dim(prompt_state, prompt_slot, 0, keepdims=False)

        def advance(carried_state, inputs_now):
            decay_now, size_now, input_now, b_now, c_now = inputs_now
            carried_state = decay_now[:, None, None] * carried_state + size_now[:, None, None] * input_now[:, :, None] * b_now[None, None, :]
            output_now = jnp.einsum('hdn,n->hd', carried_state, c_now, precision=lax.Precision.HIGHEST) + skip_d[:, None] * input_now
            return (carried_state, (carried_state, output_now))
        last_state, (all_states, ssm_out) = lax.scan(advance, initial, (decay, step_size, heads_x, b_part, c_part))
        kept_state_r = lax.dynamic_index_in_dim(all_states, accepted_r - 1, 0, keepdims=False)
        gated = (ssm_out.reshape(DRAFT, SSM_INNER) * jax.nn.silu(gate_r.astype(jnp.float32))).astype(jnp.bfloat16)
        edge_rows = jnp.concatenate([series_x, series_bc], axis=1)
        kept_conv_r = lax.dynamic_slice_in_dim(edge_rows, accepted_r, CONV - 1, 0).astype(jnp.bfloat16)
        return (attended, gated, kept_state_r, kept_conv_r)
    attended_all, gated_all, kept_state, kept_conv = lax.map(one_request, (queries, key_value, slots, accepted, gate_z, ssm_in, bc_in, dt_in))
    mixer = jnp.dot(attended_all.reshape(TOKENS, Q_HEADS * HEAD_DIM), w_attn_out, preferred_element_type=jnp.float32)
    mixer = mixer + jnp.dot(gated_all.reshape(TOKENS, SSM_INNER), w_mamba_out, preferred_element_type=jnp.float32)
    after_mixer = (flat_rows.astype(jnp.float32) + mixer).astype(jnp.bfloat16)
    prepared = rms_scale(after_mixer, mlp_gain).astype(jnp.bfloat16)
    gate_val = jnp.dot(prepared, w_gate, preferred_element_type=jnp.float32)
    up_val = jnp.dot(prepared, w_up, preferred_element_type=jnp.float32)
    active = (jax.nn.silu(gate_val) * up_val).astype(jnp.bfloat16)
    block_units = FF // N_REQ

    def add_block(running_sum, block_index):
        first_unit = (block_index * block_units).astype(jnp.int32)
        active_block = lax.dynamic_slice_in_dim(active, first_unit, block_units, 1)
        down_block = lax.dynamic_slice_in_dim(w_down, first_unit, block_units, 0)
        feed_part = jnp.dot(active_block, down_block, preferred_element_type=jnp.float32)
        feed_part = lax.optimization_barrier(feed_part.astype(jnp.bfloat16)).astype(jnp.float32)
        return (running_sum + feed_part, None)
    feed_total, unused_out = lax.scan(add_block, jnp.zeros((TOKENS, D), jnp.float32), jnp.arange(N_REQ, dtype=jnp.int32))
    hidden_out = (after_mixer.astype(jnp.float32) + feed_total).astype(jnp.bfloat16)
    final_rows = rms_scale(hidden_out, final_gain).astype(jnp.bfloat16)
    next_ids = jnp.concatenate([draft_ids[:, 1:], draft_ids[:, :1]], axis=1).reshape(TOKENS).astype(jnp.int32)
    position = (jnp.arange(TOKENS) % DRAFT).astype(jnp.int32)
    block_rows = ROW_REQ * DRAFT

    def score_block(inputs):
        rows_block, ids_block, position_block = inputs
        logits = lax.dot_general(rows_block, head_weight, (((1,), (1,)), ((), ())), preferred_element_type=jnp.float32)
        logit_top = lax.optimization_barrier(jnp.max(logits, axis=1))
        log_total = logit_top + jnp.log(lax.optimization_barrier(jnp.sum(jnp.exp(logits - logit_top[:, None]), axis=1)))
        target = jnp.take_along_axis(logits, ids_block[:, None], axis=1)[:, 0]
        return jnp.where(position_block < DRAFT - 1, target - log_total, logit_top - log_total)
    verify_scores = lax.map(score_block, (final_rows.reshape(TOKENS // block_rows, block_rows, D), next_ids.reshape(TOKENS // block_rows, block_rows), position.reshape(TOKENS // block_rows, block_rows)))
    return (hidden_out.reshape(REQS, DRAFT, D), verify_scores.reshape(REQS, DRAFT), kept_state, kept_conv)
```

```python
import functools

import jax
import jax.numpy as jnp
from jax import lax
from jax.experimental import pallas as pl
from jax.experimental.pallas import tpu as pltpu
from jax.sharding import PartitionSpec as P

Q_HEADS = 8
KV_HEADS = 2
HEAD_DIM = 128
SSM_DIM = 64
STATE = 256
CONV = 4
PROMPTS = 2
P_MAX = 1024
DRAFT = 16
MESH = pl.DeviceIdType.MESH


eps_norm = 1e-05
far_below = -1e30


def rms_scale(values, gain):
    widened = values.astype(jnp.float32)
    spread = jnp.mean(widened * widened, axis=-1, keepdims=True)
    return widened * lax.rsqrt(spread + eps_norm) * gain.astype(jnp.float32)


def convolve(series, kernel, length):
    summed = jnp.zeros(series.shape[:-2] + (length, series.shape[-1]), jnp.float32)
    for kernel_tap in range(kernel.shape[0]):
        window = lax.slice_in_dim(series, kernel_tap, kernel_tap + length, axis=series.ndim - 2)
        summed = summed + window * kernel[kernel_tap].astype(jnp.float32)
    return jax.nn.silu(summed)


def tail_kernel(
    n,
    m,
    mixed_ref,
    hidden_ref,
    mlp_gain_ref,
    final_gain_ref,
    ids_ref,
    gate_hbm,
    up_hbm,
    down_hbm,
    head_hbm,
    kept_hbm,
    edge_hbm,
    hidden_out_ref,
    verify_ref,
    kept_out,
    edge_out,
    gate_w,
    up_w,
    down_w,
    head_w,
    after_ref,
    mix_in,
    rows_ref,
    final_ref,
    final_t,
    active_ref,
    down_ref,
    pair_in,
    chip_send,
    chip_in,
    stats_ref,
    load_sems,
    mix_sems,
    gather_sems,
    final_sems,
    pair_sems,
    chip_sems,
    stats_sems,
    kept_sems,
    edge_sems,
):
    req = lax.axis_index("req")
    mdl = lax.axis_index("mdl")
    chips = n // 2
    chip = req // 2
    core = req % 2
    sibling = chip * 2 + (1 - core)
    block = after_ref.shape[0]
    width = after_ref.shape[1]
    tokens = n * block
    own_reqs = kept_out.shape[0]
    heads = kept_hbm.shape[1]

    loads = [
        pltpu.make_async_copy(src, dst, load_sems.at[i])
        for i, (src, dst) in enumerate(
            ((gate_hbm, gate_w), (up_hbm, up_w), (down_hbm, down_w), (head_hbm, head_w))
        )
    ]
    for load in loads:
        load.start()

    barrier = pltpu.get_barrier_semaphore()
    for d in range(1, m):
        pl.semaphore_signal(
            barrier, inc=1, device_id=(req, (mdl + d) % m), device_id_type=MESH
        )
    for d in range(1, n):
        pl.semaphore_signal(
            barrier, inc=1, device_id=((req + d) % n, mdl), device_id_type=MESH
        )
    pl.semaphore_wait(barrier, m - 1 + n - 1)

    def send(src, dst, sems, index, device):
        copy = pltpu.make_async_remote_copy(
            src_ref=src,
            dst_ref=dst,
            send_sem=sems.at[0, index],
            recv_sem=sems.at[1, index],
            device_id=device,
            device_id_type=MESH,
        )
        copy.start()
        return copy

    mixes = []
    for d in range(1, m):
        to = (mdl + d) % m
        mixes.append(
            send(
                mixed_ref.at[pl.ds(to * block, block)],
                mix_in.at[d - 1],
                mix_sems,
                d - 1,
                (req, to),
            )
        )
    total = mixed_ref[pl.ds(mdl * block, block)].astype(jnp.float32)
    for copy in mixes:
        copy.wait_recv()
    for d in range(m - 1):
        total = total + mix_in[d].astype(jnp.float32)
    after = (
        hidden_ref[pl.ds(mdl * block, block)].astype(jnp.float32) + total
    ).astype(jnp.bfloat16)
    after_ref[...] = after
    rows_ref[req] = rms_scale(after, mlp_gain_ref[...]).astype(jnp.bfloat16)

    def gather_rows(buffer, sems):
        sent = [send(buffer.at[req], buffer.at[req], sems, 0, (sibling, mdl))]
        across = []
        for c in range(1, chips):
            to = (chip + c) % chips * 2 + core
            across.append(send(buffer.at[req], buffer.at[req], sems, c, (to, mdl)))
        for c in range(1, chips):
            across[c - 1].wait_recv()
            source = (chip + chips - c) % chips * 2 + core
            sent.append(
                send(buffer.at[source], buffer.at[source], sems, chips - 1 + c, (sibling, mdl))
            )
        for copy in sent:
            copy.wait_recv()
        return sent + across

    waits = gather_rows(rows_ref, gather_sems)

    moves = []
    for d in range(1, m):
        to = (mdl + d) % m
        moves.append(
            send(
                kept_hbm.at[pl.ds(to * own_reqs, own_reqs)],
                kept_out.at[:, pl.ds(mdl * heads, heads)],
                kept_sems,
                d - 1,
                (req, to),
            )
        )
        moves.append(
            send(
                edge_hbm.at[pl.ds(to * own_reqs, own_reqs)],
                edge_out.at[mdl],
                edge_sems,
                d - 1,
                (req, to),
            )
        )
    own_kept = pltpu.make_async_copy(
        kept_hbm.at[pl.ds(mdl * own_reqs, own_reqs)],
        kept_out.at[:, pl.ds(mdl * heads, heads)],
        load_sems.at[4],
    )
    own_edge = pltpu.make_async_copy(
        edge_hbm.at[pl.ds(mdl * own_reqs, own_reqs)], edge_out.at[mdl], load_sems.at[5]
    )
    own_kept.start()
    own_edge.start()

    for load in loads[:3]:
        load.wait()
    units = gate_w.shape[1]
    unit_step = min(units, 256)
    group = 256 // block
    column_step = 512

    @pl.loop(0, n // group)
    def _(part):
        first = part * group
        prepared = rows_ref[pl.ds(first, group)].reshape(256, width)

        @pl.loop(0, units // unit_step)
        def _(step):
            at = pl.ds(pl.multiple_of(step * unit_step, unit_step), unit_step)
            gate_val = jnp.dot(prepared, gate_w[:, at], preferred_element_type=jnp.float32)
            up_val = jnp.dot(prepared, up_w[:, at], preferred_element_type=jnp.float32)
            active_ref[:, at] = (jax.nn.silu(gate_val) * up_val).astype(jnp.bfloat16)

        @pl.loop(0, width // column_step)
        def _(step):
            at = pl.ds(pl.multiple_of(step * column_step, column_step), column_step)
            value = jnp.dot(active_ref[...], down_w[:, at], preferred_element_type=jnp.float32)
            down_ref[pl.ds(first, group), :, at] = value.astype(jnp.bfloat16).reshape(
                group, block, column_step
            )

    pairs = []
    for c in range(chips):
        to_chip = (chip + 1 + c) % chips
        pairs.append(
            send(
                down_ref.at[to_chip * 2 + (1 - core)],
                pair_in.at[c],
                pair_sems,
                c,
                (sibling, mdl),
            )
        )
    for c in range(chips - 1):
        to = (chip + 1 + c) % chips * 2 + core
        pairs[c].wait_recv()
        chip_send[c] = (
            down_ref[to].astype(jnp.float32) + pair_in[c].astype(jnp.float32)
        ).astype(jnp.bfloat16)
        waits.append(send(chip_send.at[c], chip_in.at[c], chip_sems, c, (to, mdl)))
    pairs[chips - 1].wait_recv()
    summed = down_ref[req].astype(jnp.float32) + pair_in[chips - 1].astype(jnp.float32)
    for c in range(chips - 1):
        waits[-(chips - 1) + c].wait_recv()
        summed = summed + chip_in[c].astype(jnp.float32)
    result = (after_ref[...].astype(jnp.float32) + summed).astype(jnp.bfloat16)
    hidden_out_ref[...] = result
    final_ref[req] = rms_scale(result, final_gain_ref[...]).astype(jnp.bfloat16)
    waits += pairs
    waits += gather_rows(final_ref, final_sems)

    @pl.loop(0, width // 256)
    def _(step):
        at = pl.ds(pl.multiple_of(step * 256, 256), 256)
        final_t[at, :] = (
            final_ref[:, :, at].reshape(tokens, 256).astype(jnp.float32).T.astype(jnp.bfloat16)
        )

    loads[3].wait()
    vocab_here = head_w.shape[0]
    vocab_step = 512
    ids = ids_ref[0:1, :]
    start = (
        jnp.full((1, tokens), far_below, jnp.float32),
        jnp.zeros((1, tokens), jnp.float32),
        jnp.zeros((1, tokens), jnp.float32),
    )

    def head_step(step, carry):
        top, weight, target = carry
        first = pl.multiple_of(step * vocab_step, vocab_step)
        logits = jnp.dot(
            head_w[pl.ds(first, vocab_step), :], final_t[...], preferred_element_type=jnp.float32
        )
        vocab_ids = (
            req * vocab_here + first + lax.broadcasted_iota(jnp.int32, (vocab_step, tokens), 0)
        )
        target = target + jnp.sum(
            jnp.where(vocab_ids == ids, logits, 0.0), axis=0, keepdims=True
        )
        new_top = jnp.maximum(top, jnp.max(logits, axis=0, keepdims=True))
        weight = weight * jnp.exp(top - new_top) + jnp.sum(
            jnp.exp(logits - new_top), axis=0, keepdims=True
        )
        return (new_top, weight, target)

    top, weight, target = lax.fori_loop(0, vocab_here // vocab_step, head_step, start)
    stats_ref[req] = jnp.concatenate(
        [top, weight, target, jnp.zeros((5, tokens), jnp.float32)], axis=0
    )
    shares = [
        send(stats_ref.at[req], stats_ref.at[req], stats_sems, d - 1, ((req + d) % n, mdl))
        for d in range(1, n)
    ]
    for copy in shares:
        copy.wait_recv()
    stats = stats_ref[...]
    tops, weights, targets = stats[:, 0:1, :], stats[:, 1:2, :], stats[:, 2:3, :]
    top = jnp.max(tops, axis=0)
    log_total = top + jnp.log(jnp.sum(weights * jnp.exp(tops - top[None]), axis=0))
    target = jnp.sum(targets, axis=0)
    position = lax.broadcasted_iota(jnp.int32, (1, tokens), 1) % DRAFT
    score = jnp.where(position < DRAFT - 1, target, top) - log_total
    verify_ref[...] = jnp.broadcast_to(score, verify_ref.shape)

    for copy in mixes + waits + shares:
        copy.wait_send()
    for copy in moves:
        copy.wait()
    own_kept.wait()
    own_edge.wait()


def run_tail(
    mixed, hidden, mlp_gain, final_gain, ids, w_gate, w_up, w_down, head_weight, kept, edges
):
    n = lax.axis_size("req")
    m = lax.axis_size("mdl")
    chips = n // 2
    row_tokens, width = hidden.shape
    block = row_tokens // m
    tokens = n * block
    row_reqs, heads = kept.shape[:2]
    own_reqs = row_reqs // m
    vmem = pl.BlockSpec(memory_space=pltpu.VMEM)
    anywhere = pl.BlockSpec(memory_space=pl.ANY)
    bf16 = jnp.bfloat16
    sems = pltpu.SemaphoreType.DMA
    return pl.pallas_call(
        functools.partial(tail_kernel, n, m),
        out_shape=(
            jax.ShapeDtypeStruct((block, width), bf16),
            jax.ShapeDtypeStruct((8, tokens), jnp.float32),
            jax.ShapeDtypeStruct((own_reqs, heads * m) + kept.shape[2:], bf16),
            jax.ShapeDtypeStruct((m, own_reqs) + edges.shape[1:], bf16),
        ),
        in_specs=[vmem] * 5 + [anywhere] * 6,
        out_specs=(vmem, vmem, anywhere, anywhere),
        scratch_shapes=[
            pltpu.VMEM(w_gate.shape, bf16),
            pltpu.VMEM(w_up.shape, bf16),
            pltpu.VMEM(w_down.shape, bf16),
            pltpu.VMEM(head_weight.shape, bf16),
            pltpu.VMEM((block, width), bf16),
            pltpu.VMEM((m - 1, block, width), bf16),
            pltpu.VMEM((n, block, width), bf16),
            pltpu.VMEM((n, block, width), bf16),
            pltpu.VMEM((width, tokens), bf16),
            pltpu.VMEM((256, w_gate.shape[1]), bf16),
            pltpu.VMEM((n, block, width), bf16),
            pltpu.VMEM((chips, block, width), bf16),
            pltpu.VMEM((chips - 1, block, width), bf16),
            pltpu.VMEM((chips - 1, block, width), bf16),
            pltpu.VMEM((n, 8, tokens), jnp.float32),
            sems((6,)),
            sems((2, m - 1)),
            sems((2, 2 * chips - 1)),
            sems((2, 2 * chips - 1)),
            sems((2, chips)),
            sems((2, chips - 1)),
            sems((2, n - 1)),
            sems((2, m - 1)),
            sems((2, m - 1)),
        ],
        compiler_params=pltpu.CompilerParams(
            collective_id=0, has_side_effects=True, vmem_limit_bytes=50 * 1024 * 1024
        ),
    )(mixed, hidden, mlp_gain, final_gain, ids, w_gate, w_up, w_down, head_weight, kept, edges)


def shards(
    hidden_in,
    mixer_gain,
    w_query,
    w_kv,
    w_attn_out,
    prompt_kv,
    prompt_lengths,
    member,
    accepted,
    w_z,
    w_x,
    w_bc,
    w_dt,
    conv_x,
    conv_bc,
    ssm_rate,
    dt_bias,
    skip_d,
    prompt_state,
    prompt_conv_x,
    prompt_conv_bc,
    w_mamba_out,
    mlp_gain,
    w_gate,
    w_up,
    w_down,
    final_gain,
    head_weight,
    draft_ids,
):
    row_reqs, draft_len, width = hidden_in.shape
    mdl_count = lax.axis_size("mdl")
    req_count = lax.axis_size("req")
    mdl_rank = lax.axis_index("mdl")
    req_rank = lax.axis_index("req")
    row_tokens = row_reqs * draft_len
    own_reqs = row_reqs // mdl_count
    own_tokens = own_reqs * draft_len
    contract_last = (((1,), (1,)), ((), ()))
    flat_rows = hidden_in.reshape(row_tokens, width)
    normed = rms_scale(flat_rows, mixer_gain).astype(jnp.bfloat16)
    token_request = jnp.arange(row_tokens) // draft_len
    token_position = jnp.arange(row_tokens) % draft_len
    prompt_pick = jax.nn.one_hot(member, PROMPTS, dtype=jnp.float32)
    local_heads = w_query.shape[1] // HEAD_DIM
    per_group = Q_HEADS // KV_HEADS
    kv_index = mdl_rank * local_heads // per_group
    kv_weight = lax.dynamic_index_in_dim(w_kv, kv_index, 0, keepdims=False)
    queries = jnp.dot(normed, w_query, preferred_element_type=jnp.float32).astype(jnp.bfloat16)
    key_value = jnp.dot(normed, kv_weight, preferred_element_type=jnp.float32).astype(jnp.bfloat16)
    draft_keys = key_value[:, :HEAD_DIM]
    draft_values = key_value[:, HEAD_DIM:]
    query_rows = (
        queries.reshape(row_tokens, local_heads, HEAD_DIM)
        .transpose(1, 0, 2)
        .reshape(local_heads * row_tokens, HEAD_DIM)
    )
    row_request = jnp.tile(token_request, local_heads)
    row_position = jnp.tile(token_position, local_heads)
    row_member = jnp.take(member, row_request)
    cached = lax.dynamic_index_in_dim(prompt_kv, kv_index, 1, keepdims=False)
    score_scale = HEAD_DIM ** (-0.5)
    draft_scores = (
        lax.dot_general(query_rows, draft_keys, contract_last, preferred_element_type=jnp.float32)
        * score_scale
    )
    draft_mask = (row_request[:, None] == token_request[None, :]) & (
        token_position[None, :] <= row_position[:, None]
    )
    draft_top = jnp.max(jnp.where(draft_mask, draft_scores, far_below), axis=1)

    def prompt_scores(prompt_slot, row_count):
        key_block = cached[prompt_slot]
        scores = (
            lax.dot_general(
                query_rows,
                key_block[:, :HEAD_DIM],
                contract_last,
                preferred_element_type=jnp.float32,
            )
            * score_scale
        )
        positions = jnp.arange(row_count)
        valid_keys = (row_member[:, None] == prompt_slot) & (
            positions[None, :] < prompt_lengths[prompt_slot]
        )
        return (scores, valid_keys, key_block[:, HEAD_DIM:])

    def add_weights(carry, scores, valid_keys, values_block, row_top):
        weight_total, weighted = carry
        weights = jnp.exp(jnp.where(valid_keys, scores - row_top[:, None], far_below))
        weight_total = weight_total + jnp.sum(weights, axis=1)
        weighted = weighted + jnp.dot(
            weights.astype(jnp.bfloat16), values_block, preferred_element_type=jnp.float32
        )
        return (weight_total, weighted)

    row_top = draft_top
    prompt_parts = []
    for prompt_slot in range(PROMPTS):
        scores, valid_keys, values_block = prompt_scores(prompt_slot, P_MAX)
        row_top = jnp.maximum(row_top, jnp.max(jnp.where(valid_keys, scores, far_below), axis=1))
        prompt_parts.append((scores, valid_keys, values_block))
    carry = (
        jnp.zeros(row_top.shape, jnp.float32),
        jnp.zeros((query_rows.shape[0], HEAD_DIM), jnp.float32),
    )
    for scores, valid_keys, values_block in prompt_parts:
        carry = add_weights(carry, scores, valid_keys, values_block, row_top)
    carry = add_weights(carry, draft_scores, draft_mask, draft_values, row_top)
    attended = (carry[1] / carry[0][:, None]).astype(jnp.bfloat16)
    attention_flat = (
        attended.reshape(local_heads, row_tokens, HEAD_DIM)
        .transpose(1, 0, 2)
        .reshape(row_tokens, local_heads * HEAD_DIM)
    )
    gate_z = jnp.dot(normed, w_z, preferred_element_type=jnp.float32).astype(jnp.bfloat16)
    ssm_in = jnp.dot(normed, w_x, preferred_element_type=jnp.float32).astype(jnp.bfloat16)
    bc_in = jnp.dot(normed, w_bc, preferred_element_type=jnp.float32).astype(jnp.bfloat16)
    dt_in = jnp.dot(normed, w_dt, preferred_element_type=jnp.float32).astype(jnp.bfloat16)
    local_inner = w_x.shape[1]
    local_ssm = local_inner // SSM_DIM
    edge_len = CONV - 1
    start_x = jnp.einsum(
        "rp,pcw->rcw",
        prompt_pick,
        prompt_conv_x.astype(jnp.float32),
        precision=lax.Precision.HIGHEST,
    )
    start_bc = jnp.einsum(
        "rp,pcw->rcw",
        prompt_pick,
        prompt_conv_bc.astype(jnp.float32),
        precision=lax.Precision.HIGHEST,
    )
    series_x = jnp.concatenate(
        [start_x, ssm_in.astype(jnp.float32).reshape(row_reqs, draft_len, local_inner)], axis=1
    )
    series_bc = jnp.concatenate(
        [start_bc, bc_in.astype(jnp.float32).reshape(row_reqs, draft_len, 2 * STATE)], axis=1
    )
    conv_xs = convolve(series_x, conv_x, draft_len)
    conv_bcs = convolve(series_bc, conv_bc, draft_len)
    b_part = conv_bcs[:, :, :STATE]
    c_part = conv_bcs[:, :, STATE:]
    step_size = jax.nn.softplus(
        dt_in.astype(jnp.float32).reshape(row_reqs, draft_len, local_ssm) + dt_bias
    )
    log_decay = jnp.cumsum(-step_size * ssm_rate, axis=1)
    heads_x = conv_xs.reshape(row_reqs, draft_len, local_ssm, SSM_DIM)
    causal_pairs = jnp.arange(draft_len)[:, None] >= jnp.arange(draft_len)[None, :]
    log_gaps = log_decay[:, :, None, :] - log_decay[:, None, :, :]
    mixing = jnp.exp(jnp.where(causal_pairs[None, :, :, None], log_gaps, far_below))
    intersection = jnp.einsum("rtn,rsn->rts", c_part, b_part, precision=lax.Precision.HIGHEST)
    pair_weights = mixing * intersection[..., None] * step_size[:, None, :, :]
    intra = jnp.einsum("rtsh,rshp->rthp", pair_weights, heads_x, precision=lax.Precision.HIGHEST)
    initial = jnp.einsum(
        "rp,phdn->rhdn", prompt_pick, prompt_state, precision=lax.Precision.HIGHEST
    )
    carried = (
        jnp.einsum("rhdn,rtn->rthd", initial, c_part, precision=lax.Precision.HIGHEST)
        * jnp.exp(log_decay)[..., None]
    )
    ssm_out = intra + carried + skip_d[None, None, :, None] * heads_x
    gated = (
        ssm_out.reshape(row_tokens, local_inner) * jax.nn.silu(gate_z.astype(jnp.float32))
    ).astype(jnp.bfloat16)
    last_index = accepted - 1
    pick_step = jax.nn.one_hot(last_index, draft_len, dtype=jnp.float32)
    final_log = jnp.einsum("rt,rth->rh", pick_step, log_decay, precision=lax.Precision.HIGHEST)
    upto_last = jnp.arange(draft_len)[None, :] <= last_index[:, None]
    carry_weights = (
        jnp.exp(jnp.where(upto_last[:, :, None], final_log[:, None, :] - log_decay, far_below))
        * step_size
    )
    kept_states = jnp.exp(final_log)[:, :, None, None] * initial
    kept_states = kept_states + jnp.einsum(
        "rsh,rshd,rsn->rhdn", carry_weights, heads_x, b_part, precision=lax.Precision.HIGHEST
    )
    window_pick = jax.nn.one_hot(
        accepted[:, None] + jnp.arange(edge_len)[None, :], edge_len + draft_len, dtype=jnp.float32
    )
    kept_x = jnp.einsum("rkl,rlc->rkc", window_pick, series_x, precision=lax.Precision.HIGHEST)
    kept_bc = jnp.einsum("rkl,rlc->rkc", window_pick, series_bc, precision=lax.Precision.HIGHEST)
    edges = jnp.pad(kept_x.astype(jnp.bfloat16), ((0, 0), (0, 16 - edge_len), (0, 0)))
    mixed = (
        jnp.dot(attention_flat, w_attn_out, preferred_element_type=jnp.float32)
        + jnp.dot(gated, w_mamba_out, preferred_element_type=jnp.float32)
    ).astype(jnp.bfloat16)
    id_grid = draft_ids.reshape(req_count, mdl_count, own_reqs, draft_len)
    column_ids = lax.dynamic_index_in_dim(id_grid, mdl_rank, 1, keepdims=False)
    next_ids = jnp.concatenate([column_ids[..., 1:], column_ids[..., :1]], axis=-1).reshape(1, -1)
    hidden_out, scores_all, kept_all, edges_all = run_tail(
        mixed,
        flat_rows,
        mlp_gain.reshape(1, width),
        final_gain.reshape(1, width),
        jnp.broadcast_to(next_ids, (8, next_ids.shape[1])),
        w_gate,
        w_up,
        w_down,
        head_weight,
        kept_states.astype(jnp.bfloat16),
        edges,
    )
    kept_state = kept_all.astype(jnp.float32)
    edge_x = (
        edges_all[:, :, :edge_len]
        .transpose(1, 2, 0, 3)
        .reshape(own_reqs, edge_len, mdl_count * local_inner)
    )
    own_bc = lax.dynamic_slice_in_dim(kept_bc, mdl_rank * own_reqs, own_reqs, 0)
    kept_conv = jnp.concatenate([edge_x, own_bc.astype(jnp.bfloat16)], axis=2)
    verify_scores = lax.dynamic_slice_in_dim(
        scores_all[0], req_rank * own_tokens, own_tokens, 0
    ).reshape(own_reqs, draft_len)
    return (hidden_out.reshape(own_reqs, draft_len, width), verify_scores, kept_state, kept_conv)


def solution(mesh):
    in_specs = (
        P("req", None, None),
        P(),
        P(None, "mdl"),
        P(),
        P("mdl", None),
        P("req", None, None, None),
        P("req"),
        P("req"),
        P("req"),
        P(None, "mdl"),
        P(None, "mdl"),
        P(),
        P(None, "mdl"),
        P(None, "mdl"),
        P(),
        P("mdl"),
        P("mdl"),
        P("mdl"),
        P("req", "mdl", None, None),
        P("req", None, "mdl"),
        P("req", None, None),
        P("mdl", None),
        P(),
        P(None, "req"),
        P(None, "req"),
        P("req", None),
        P(),
        P("req", None),
        P(),
    )
    out_specs = (
        P(("req", "mdl"), None, None),
        P(("req", "mdl"), None),
        P(("req", "mdl"), None, None, None),
        P(("req", "mdl"), None, None),
    )
    return jax.shard_map(shards, mesh=mesh, in_specs=in_specs, out_specs=out_specs, check_vma=False)
```

```python
import functools

import jax
import jax.numpy as jnp
from jax import lax
from jax.experimental import pallas as pl
from jax.experimental.pallas import tpu as pltpu
from jax.sharding import PartitionSpec as P

Q_HEADS = 8
KV_HEADS = 2
HEAD_DIM = 128
SSM_DIM = 64
STATE = 256
CONV = 4
PROMPTS = 2
P_MAX = 1024
DRAFT = 16
MESH = pl.DeviceIdType.MESH


eps_norm = 1e-05
far_below = -1e30


def rms_scale(values, gain):
    widened = values.astype(jnp.float32)
    spread = jnp.mean(widened * widened, axis=-1, keepdims=True)
    return widened * lax.rsqrt(spread + eps_norm) * gain.astype(jnp.float32)


def dot(a, b):
    return jnp.dot(a, b, preferred_element_type=jnp.float32)


def dot_rows(a, b):
    return lax.dot_general(a, b, (((1,), (1,)), ((), ())), preferred_element_type=jnp.float32)


def dot_exact(a, b):
    return jnp.dot(
        a, b, preferred_element_type=jnp.float32, precision=lax.Precision.HIGHEST
    )


def ones_where(mask, dtype=jnp.bfloat16):
    return jnp.where(mask, 1.0, 0.0).astype(dtype)


def mixer_kernel(
    m,
    member_ref,
    lengths_ref,
    accepted_ref,
    hidden_ref,
    gain_ref,
    w_dt_ref,
    conv_x_ref,
    conv_bc_ref,
    rows_x_ref,
    rows_bc_ref,
    head_params_ref,
    w_query_hbm,
    w_kv_hbm,
    prompt_kv_hbm,
    w_z_hbm,
    w_x_hbm,
    w_bc_hbm,
    state_hbm,
    w_attn_hbm,
    w_mamba_hbm,
    mixed_ref,
    kept_ref,
    edge_x_ref,
    edge_bc_ref,
    w_query,
    w_kv,
    prompt_kv,
    w_z,
    w_x,
    w_bc,
    state,
    w_attn,
    w_mamba,
    normed_ref,
    load_sems,
):
    mdl = lax.axis_index("mdl")
    local_heads = w_query.shape[1] // HEAD_DIM
    group = mdl * local_heads // (Q_HEADS // KV_HEADS)
    pairs = (
        (w_x_hbm, w_x),
        (w_bc_hbm, w_bc),
        (w_z_hbm, w_z),
        (w_query_hbm, w_query),
        (w_kv_hbm.at[group], w_kv),
        (state_hbm, state),
        (prompt_kv_hbm.at[:, group], prompt_kv),
        (w_attn_hbm, w_attn),
        (w_mamba_hbm, w_mamba),
    )
    loads = [
        pltpu.make_async_copy(src, dst, load_sems.at[i]) for i, (src, dst) in enumerate(pairs)
    ]
    for load in loads:
        load.start()

    tokens, width = hidden_ref.shape
    reqs = tokens // DRAFT
    inner = w_x.shape[1]
    heads = inner // SSM_DIM
    edge = CONV - 1
    bf16, f32 = jnp.bfloat16, jnp.float32
    token = lax.broadcasted_iota(jnp.int32, (tokens, 1), 0)
    request, position = token // DRAFT, token % DRAFT
    other = lax.broadcasted_iota(jnp.int32, (1, tokens), 1)
    other_request, other_position = other // DRAFT, other % DRAFT
    member = jnp.zeros((tokens, 1), jnp.int32)
    accepted = jnp.zeros((tokens, 1), jnp.int32)
    for r in range(reqs):
        member = jnp.where(request == r, member_ref[r], member)
        accepted = jnp.where(request == r, accepted_ref[r], accepted)
    first_prompt = member == 0
    valid = jnp.where(first_prompt, lengths_ref[0], lengths_ref[1])
    same = request == other_request
    causal = same & (other_position <= position)

    normed_ref[...] = rms_scale(hidden_ref[...], gain_ref[...]).astype(bf16)
    normed = normed_ref[...]
    dt_in = dot(normed, w_dt_ref[...]).astype(bf16)
    loads[0].wait()
    ssm_in = dot(normed, w_x[...]).astype(bf16)
    loads[1].wait()
    bc_in = dot(normed, w_bc[...]).astype(bf16)

    row_at = lax.broadcasted_iota(jnp.int32, (1, rows_x_ref.shape[0]), 1)
    rows_x, rows_bc = rows_x_ref[...], rows_bc_ref[...]
    keep = position < edge
    kept_at = accepted + position
    pick_drafts = ones_where(same & keep & (other_position == kept_at - edge))
    pick_prompt = ones_where((row_at == member * edge + kept_at) & (kept_at < edge) & keep)
    edge_x_ref[...] = (dot(pick_drafts, ssm_in) + dot(pick_prompt, rows_x)).astype(bf16)
    edge_bc_ref[...] = (dot(pick_drafts, bc_in) + dot(pick_prompt, rows_bc)).astype(bf16)

    def convolved(series, rows, taps):
        wide = series.astype(f32)
        total = wide * taps[edge : edge + 1].astype(f32)
        for back in range(1, CONV):
            shifted = jnp.where(position >= back, pltpu.roll(wide, back, 0), 0.0)
            begin = ones_where(
                (row_at == member * edge + edge + position - back) & (position < back)
            )
            shifted = shifted + dot(begin, rows)
            total = total + shifted * taps[edge - back : edge - back + 1].astype(f32)
        return jax.nn.silu(total)

    x = convolved(ssm_in, rows_x, conv_x_ref[...])
    bc = convolved(bc_in, rows_bc, conv_bc_ref[...])
    b_part = bc[:, :STATE].astype(bf16)
    c_part = bc[:, STATE:].astype(bf16)

    head_row = lax.broadcasted_iota(jnp.int32, (dt_in.shape[1], inner), 0)
    head_col = lax.broadcasted_iota(jnp.int32, (dt_in.shape[1], inner), 1)
    spread = ones_where(head_row == head_col // SSM_DIM)
    dt_bias = head_params_ref[0:1, :]
    rate = head_params_ref[1:2, :]
    skip = head_params_ref[2:3, :]
    raw = dot(dt_in, spread) + dt_bias
    step_size = jnp.maximum(raw, 0.0) + jnp.log1p(jnp.exp(-jnp.abs(raw)))
    log_decay = dot_exact(ones_where(causal, f32), -step_size * rate)
    log_rows = log_decay.T
    last = accepted - 1
    final_log = dot_exact(ones_where(same & (other_position == last), f32), log_decay)
    final_rows = jnp.exp(final_log.T)
    carry = jnp.exp(jnp.where(position <= last, final_log - log_decay, far_below)) * step_size
    carried_t = (carry * x).T.astype(bf16)

    loads[5].wait()
    flat = (inner, STATE)
    first_state, second_state = state[0].reshape(flat), state[1].reshape(flat)
    for r in range(reqs):
        own = jnp.where(request == r, b_part, jnp.zeros_like(b_part))
        begin = jnp.where(
            jnp.broadcast_to(member_ref[r], (1, STATE)) == 0, first_state, second_state
        )
        kept = final_rows[:, r * DRAFT : r * DRAFT + 1] * begin + dot(carried_t, own)
        kept_ref[r] = kept.astype(bf16).reshape(heads, SSM_DIM, STATE)

    initial = jnp.where(
        first_prompt,
        dot_rows(c_part, first_state.astype(bf16)),
        dot_rows(c_part, second_state.astype(bf16)),
    )
    overlap = dot_rows(c_part, b_part)
    stepped = (step_size * x).astype(bf16)
    intra = []
    for h in range(heads):
        at = h * SSM_DIM
        gaps = log_decay[:, at : at + 1] - log_rows[at : at + 1, :]
        mixing = jnp.exp(jnp.where(causal, gaps, far_below)) * overlap
        intra.append(dot(mixing.astype(bf16), stepped[:, at : at + SSM_DIM]))
    ssm_out = jnp.concatenate(intra, axis=1) + initial * jnp.exp(log_decay) + skip * x
    loads[2].wait()
    gate_z = dot(normed, w_z[...]).astype(bf16).astype(f32)
    gated = (ssm_out * jax.nn.silu(gate_z)).astype(bf16)

    loads[3].wait()
    queries = dot(normed, w_query[...]).astype(bf16)
    loads[4].wait()
    key_value = dot(normed, w_kv[...]).astype(bf16)
    loads[6].wait()
    scale = HEAD_DIM ** (-0.5)
    usable = lax.broadcasted_iota(jnp.int32, (1, P_MAX), 1) < valid
    attended = []
    for h in range(local_heads):
        query = queries[:, h * HEAD_DIM : (h + 1) * HEAD_DIM]
        scores = jnp.where(
            first_prompt,
            dot_rows(query, prompt_kv[0, :, :HEAD_DIM]),
            dot_rows(query, prompt_kv[1, :, :HEAD_DIM]),
        )
        scores = jnp.where(usable, scores * scale, far_below)
        drafts = jnp.where(causal, dot_rows(query, key_value[:, :HEAD_DIM]) * scale, far_below)
        top = jnp.maximum(
            jnp.max(scores, axis=1, keepdims=True), jnp.max(drafts, axis=1, keepdims=True)
        )
        weights = jnp.exp(scores - top)
        draft_weights = jnp.exp(drafts - top)
        denominator = jnp.sum(weights, axis=1, keepdims=True) + jnp.sum(
            draft_weights, axis=1, keepdims=True
        )
        rounded = weights.astype(bf16)
        summed = jnp.where(
            first_prompt,
            dot(rounded, prompt_kv[0, :, HEAD_DIM:]),
            dot(rounded, prompt_kv[1, :, HEAD_DIM:]),
        ) + dot(draft_weights.astype(bf16), key_value[:, HEAD_DIM:])
        attended.append((summed / denominator).astype(bf16))
    attended = jnp.concatenate(attended, axis=1)
    loads[7].wait()
    loads[8].wait()
    for first in range(0, width, 512):
        at = slice(first, first + 512)
        mixed_ref[:, at] = (dot(attended, w_attn[:, at]) + dot(gated, w_mamba[:, at])).astype(bf16)


def run_mixers(
    member,
    lengths,
    accepted,
    hidden,
    gain,
    w_dt,
    conv_x,
    conv_bc,
    rows_x,
    rows_bc,
    head_params,
    w_query,
    w_kv,
    prompt_kv,
    w_z,
    w_x,
    w_bc,
    state,
    w_attn,
    w_mamba,
):
    m = lax.axis_size("mdl")
    tokens, width = hidden.shape
    reqs = tokens // DRAFT
    smem = pl.BlockSpec(memory_space=pltpu.SMEM)
    vmem = pl.BlockSpec(memory_space=pltpu.VMEM)
    anywhere = pl.BlockSpec(memory_space=pl.ANY)
    bf16 = jnp.bfloat16
    return pl.pallas_call(
        functools.partial(mixer_kernel, m),
        out_shape=(
            jax.ShapeDtypeStruct((tokens, width), bf16),
            jax.ShapeDtypeStruct((reqs,) + state.shape[1:], bf16),
            jax.ShapeDtypeStruct((tokens, w_x.shape[1]), bf16),
            jax.ShapeDtypeStruct((tokens, w_bc.shape[1]), bf16),
        ),
        in_specs=[smem] * 3 + [vmem] * 8 + [anywhere] * 9,
        out_specs=(vmem,) * 4,
        scratch_shapes=[
            pltpu.VMEM(w_query.shape, bf16),
            pltpu.VMEM(w_kv.shape[1:], bf16),
            pltpu.VMEM((PROMPTS,) + prompt_kv.shape[2:], bf16),
            pltpu.VMEM(w_z.shape, bf16),
            pltpu.VMEM(w_x.shape, bf16),
            pltpu.VMEM(w_bc.shape, bf16),
            pltpu.VMEM(state.shape, jnp.float32),
            pltpu.VMEM(w_attn.shape, bf16),
            pltpu.VMEM(w_mamba.shape, bf16),
            pltpu.VMEM((tokens, width), bf16),
            pltpu.SemaphoreType.DMA((9,)),
        ],
        compiler_params=pltpu.CompilerParams(vmem_limit_bytes=40 * 1024 * 1024),
    )(
        member,
        lengths,
        accepted,
        hidden,
        gain,
        w_dt,
        conv_x,
        conv_bc,
        rows_x,
        rows_bc,
        head_params,
        w_query,
        w_kv,
        prompt_kv,
        w_z,
        w_x,
        w_bc,
        state,
        w_attn,
        w_mamba,
    )


def tail_kernel(
    n,
    m,
    mixed_ref,
    hidden_ref,
    mlp_gain_ref,
    final_gain_ref,
    ids_ref,
    gate_hbm,
    up_hbm,
    down_hbm,
    head_hbm,
    kept_hbm,
    edge_hbm,
    hidden_out_ref,
    verify_ref,
    kept_out,
    edge_out,
    gate_w,
    up_w,
    down_w,
    head_w,
    after_ref,
    mix_in,
    rows_ref,
    final_ref,
    final_t,
    active_ref,
    down_ref,
    pair_in,
    chip_send,
    chip_in,
    stats_ref,
    load_sems,
    mix_sems,
    gather_sems,
    final_sems,
    pair_sems,
    chip_sems,
    stats_sems,
    kept_sems,
    edge_sems,
):
    req = lax.axis_index("req")
    mdl = lax.axis_index("mdl")
    chips = n // 2
    chip = req // 2
    core = req % 2
    sibling = chip * 2 + (1 - core)
    block = after_ref.shape[0]
    width = after_ref.shape[1]
    tokens = n * block
    own_reqs = kept_out.shape[0]
    heads = kept_hbm.shape[1]

    loads = [
        pltpu.make_async_copy(src, dst, load_sems.at[i])
        for i, (src, dst) in enumerate(
            ((gate_hbm, gate_w), (up_hbm, up_w), (down_hbm, down_w), (head_hbm, head_w))
        )
    ]
    for load in loads:
        load.start()

    barrier = pltpu.get_barrier_semaphore()
    for d in range(1, m):
        pl.semaphore_signal(
            barrier, inc=1, device_id=(req, (mdl + d) % m), device_id_type=MESH
        )
    for d in range(1, n):
        pl.semaphore_signal(
            barrier, inc=1, device_id=((req + d) % n, mdl), device_id_type=MESH
        )
    pl.semaphore_wait(barrier, m - 1 + n - 1)

    def send(src, dst, sems, index, device):
        copy = pltpu.make_async_remote_copy(
            src_ref=src,
            dst_ref=dst,
            send_sem=sems.at[0, index],
            recv_sem=sems.at[1, index],
            device_id=device,
            device_id_type=MESH,
        )
        copy.start()
        return copy

    mixes = []
    for d in range(1, m):
        to = (mdl + d) % m
        mixes.append(
            send(
                mixed_ref.at[pl.ds(to * block, block)],
                mix_in.at[d - 1],
                mix_sems,
                d - 1,
                (req, to),
            )
        )
    total = mixed_ref[pl.ds(mdl * block, block)].astype(jnp.float32)
    for copy in mixes:
        copy.wait_recv()
    for d in range(m - 1):
        total = total + mix_in[d].astype(jnp.float32)
    after = (
        hidden_ref[pl.ds(mdl * block, block)].astype(jnp.float32) + total
    ).astype(jnp.bfloat16)
    after_ref[...] = after
    rows_ref[req] = rms_scale(after, mlp_gain_ref[...]).astype(jnp.bfloat16)

    def gather_rows(buffer, sems):
        sent = [send(buffer.at[req], buffer.at[req], sems, 0, (sibling, mdl))]
        across = []
        for c in range(1, chips):
            to = (chip + c) % chips * 2 + core
            across.append(send(buffer.at[req], buffer.at[req], sems, c, (to, mdl)))
        for c in range(1, chips):
            across[c - 1].wait_recv()
            source = (chip + chips - c) % chips * 2 + core
            sent.append(
                send(buffer.at[source], buffer.at[source], sems, chips - 1 + c, (sibling, mdl))
            )
        for copy in sent:
            copy.wait_recv()
        return sent + across

    waits = gather_rows(rows_ref, gather_sems)

    moves = []
    for d in range(1, m):
        to = (mdl + d) % m
        moves.append(
            send(
                kept_hbm.at[pl.ds(to * own_reqs, own_reqs)],
                kept_out.at[:, pl.ds(mdl * heads, heads)],
                kept_sems,
                d - 1,
                (req, to),
            )
        )
        moves.append(
            send(
                edge_hbm.at[pl.ds(to * own_reqs, own_reqs)],
                edge_out.at[mdl],
                edge_sems,
                d - 1,
                (req, to),
            )
        )
    own_kept = pltpu.make_async_copy(
        kept_hbm.at[pl.ds(mdl * own_reqs, own_reqs)],
        kept_out.at[:, pl.ds(mdl * heads, heads)],
        load_sems.at[4],
    )
    own_edge = pltpu.make_async_copy(
        edge_hbm.at[pl.ds(mdl * own_reqs, own_reqs)], edge_out.at[mdl], load_sems.at[5]
    )
    own_kept.start()
    own_edge.start()

    for load in loads[:3]:
        load.wait()
    units = gate_w.shape[1]
    unit_step = min(units, 256)
    group = 256 // block
    column_step = 512

    @pl.loop(0, n // group)
    def _(part):
        first = part * group
        prepared = rows_ref[pl.ds(first, group)].reshape(256, width)

        @pl.loop(0, units // unit_step)
        def _(step):
            at = pl.ds(pl.multiple_of(step * unit_step, unit_step), unit_step)
            gate_val = jnp.dot(prepared, gate_w[:, at], preferred_element_type=jnp.float32)
            up_val = jnp.dot(prepared, up_w[:, at], preferred_element_type=jnp.float32)
            active_ref[:, at] = (jax.nn.silu(gate_val) * up_val).astype(jnp.bfloat16)

        @pl.loop(0, width // column_step)
        def _(step):
            at = pl.ds(pl.multiple_of(step * column_step, column_step), column_step)
            value = jnp.dot(active_ref[...], down_w[:, at], preferred_element_type=jnp.float32)
            down_ref[pl.ds(first, group), :, at] = value.astype(jnp.bfloat16).reshape(
                group, block, column_step
            )

    pairs = []
    for c in range(chips):
        to_chip = (chip + 1 + c) % chips
        pairs.append(
            send(
                down_ref.at[to_chip * 2 + (1 - core)],
                pair_in.at[c],
                pair_sems,
                c,
                (sibling, mdl),
            )
        )
    for c in range(chips - 1):
        to = (chip + 1 + c) % chips * 2 + core
        pairs[c].wait_recv()
        chip_send[c] = (
            down_ref[to].astype(jnp.float32) + pair_in[c].astype(jnp.float32)
        ).astype(jnp.bfloat16)
        waits.append(send(chip_send.at[c], chip_in.at[c], chip_sems, c, (to, mdl)))
    pairs[chips - 1].wait_recv()
    summed = down_ref[req].astype(jnp.float32) + pair_in[chips - 1].astype(jnp.float32)
    for c in range(chips - 1):
        waits[-(chips - 1) + c].wait_recv()
        summed = summed + chip_in[c].astype(jnp.float32)
    result = (after_ref[...].astype(jnp.float32) + summed).astype(jnp.bfloat16)
    hidden_out_ref[...] = result
    final_ref[req] = rms_scale(result, final_gain_ref[...]).astype(jnp.bfloat16)
    waits += pairs
    waits += gather_rows(final_ref, final_sems)

    @pl.loop(0, width // 256)
    def _(step):
        at = pl.ds(pl.multiple_of(step * 256, 256), 256)
        final_t[at, :] = (
            final_ref[:, :, at].reshape(tokens, 256).astype(jnp.float32).T.astype(jnp.bfloat16)
        )

    loads[3].wait()
    vocab_here = head_w.shape[0]
    vocab_step = 512
    ids = ids_ref[0:1, :]
    start = (
        jnp.full((1, tokens), far_below, jnp.float32),
        jnp.zeros((1, tokens), jnp.float32),
        jnp.zeros((1, tokens), jnp.float32),
    )

    def head_step(step, carry):
        top, weight, target = carry
        first = pl.multiple_of(step * vocab_step, vocab_step)
        logits = jnp.dot(
            head_w[pl.ds(first, vocab_step), :], final_t[...], preferred_element_type=jnp.float32
        )
        vocab_ids = (
            req * vocab_here + first + lax.broadcasted_iota(jnp.int32, (vocab_step, tokens), 0)
        )
        target = target + jnp.sum(
            jnp.where(vocab_ids == ids, logits, 0.0), axis=0, keepdims=True
        )
        new_top = jnp.maximum(top, jnp.max(logits, axis=0, keepdims=True))
        weight = weight * jnp.exp(top - new_top) + jnp.sum(
            jnp.exp(logits - new_top), axis=0, keepdims=True
        )
        return (new_top, weight, target)

    top, weight, target = lax.fori_loop(0, vocab_here // vocab_step, head_step, start)
    stats_ref[req] = jnp.concatenate(
        [top, weight, target, jnp.zeros((5, tokens), jnp.float32)], axis=0
    )
    shares = [
        send(stats_ref.at[req], stats_ref.at[req], stats_sems, d - 1, ((req + d) % n, mdl))
        for d in range(1, n)
    ]
    for copy in shares:
        copy.wait_recv()
    stats = stats_ref[...]
    tops, weights, targets = stats[:, 0:1, :], stats[:, 1:2, :], stats[:, 2:3, :]
    top = jnp.max(tops, axis=0)
    log_total = top + jnp.log(jnp.sum(weights * jnp.exp(tops - top[None]), axis=0))
    target = jnp.sum(targets, axis=0)
    position = lax.broadcasted_iota(jnp.int32, (1, tokens), 1) % DRAFT
    score = jnp.where(position < DRAFT - 1, target, top) - log_total
    verify_ref[...] = jnp.broadcast_to(score, verify_ref.shape)

    for copy in mixes + waits + shares:
        copy.wait_send()
    for copy in moves:
        copy.wait()
    own_kept.wait()
    own_edge.wait()


def run_tail(
    mixed, hidden, mlp_gain, final_gain, ids, w_gate, w_up, w_down, head_weight, kept, edges
):
    n = lax.axis_size("req")
    m = lax.axis_size("mdl")
    chips = n // 2
    row_tokens, width = hidden.shape
    block = row_tokens // m
    tokens = n * block
    row_reqs, heads = kept.shape[:2]
    own_reqs = row_reqs // m
    vmem = pl.BlockSpec(memory_space=pltpu.VMEM)
    anywhere = pl.BlockSpec(memory_space=pl.ANY)
    bf16 = jnp.bfloat16
    sems = pltpu.SemaphoreType.DMA
    return pl.pallas_call(
        functools.partial(tail_kernel, n, m),
        out_shape=(
            jax.ShapeDtypeStruct((block, width), bf16),
            jax.ShapeDtypeStruct((8, tokens), jnp.float32),
            jax.ShapeDtypeStruct((own_reqs, heads * m) + kept.shape[2:], bf16),
            jax.ShapeDtypeStruct((m, own_reqs) + edges.shape[1:], bf16),
        ),
        in_specs=[vmem] * 5 + [anywhere] * 6,
        out_specs=(vmem, vmem, anywhere, anywhere),
        scratch_shapes=[
            pltpu.VMEM(w_gate.shape, bf16),
            pltpu.VMEM(w_up.shape, bf16),
            pltpu.VMEM(w_down.shape, bf16),
            pltpu.VMEM(head_weight.shape, bf16),
            pltpu.VMEM((block, width), bf16),
            pltpu.VMEM((m - 1, block, width), bf16),
            pltpu.VMEM((n, block, width), bf16),
            pltpu.VMEM((n, block, width), bf16),
            pltpu.VMEM((width, tokens), bf16),
            pltpu.VMEM((256, w_gate.shape[1]), bf16),
            pltpu.VMEM((n, block, width), bf16),
            pltpu.VMEM((chips, block, width), bf16),
            pltpu.VMEM((chips - 1, block, width), bf16),
            pltpu.VMEM((chips - 1, block, width), bf16),
            pltpu.VMEM((n, 8, tokens), jnp.float32),
            sems((6,)),
            sems((2, m - 1)),
            sems((2, 2 * chips - 1)),
            sems((2, 2 * chips - 1)),
            sems((2, chips)),
            sems((2, chips - 1)),
            sems((2, n - 1)),
            sems((2, m - 1)),
            sems((2, m - 1)),
        ],
        compiler_params=pltpu.CompilerParams(
            collective_id=0, has_side_effects=True, vmem_limit_bytes=50 * 1024 * 1024
        ),
    )(mixed, hidden, mlp_gain, final_gain, ids, w_gate, w_up, w_down, head_weight, kept, edges)


def shards(
    hidden_in,
    mixer_gain,
    w_query,
    w_kv,
    w_attn_out,
    prompt_kv,
    prompt_lengths,
    member,
    accepted,
    w_z,
    w_x,
    w_bc,
    w_dt,
    conv_x,
    conv_bc,
    ssm_rate,
    dt_bias,
    skip_d,
    prompt_state,
    prompt_conv_x,
    prompt_conv_bc,
    w_mamba_out,
    mlp_gain,
    w_gate,
    w_up,
    w_down,
    final_gain,
    head_weight,
    draft_ids,
):
    row_reqs, draft_len, width = hidden_in.shape
    mdl_count = lax.axis_size("mdl")
    req_count = lax.axis_size("req")
    mdl_rank = lax.axis_index("mdl")
    req_rank = lax.axis_index("req")
    row_tokens = row_reqs * draft_len
    own_reqs = row_reqs // mdl_count
    own_tokens = own_reqs * draft_len
    flat_rows = hidden_in.reshape(row_tokens, width)
    edge_len = CONV - 1
    local_inner = w_x.shape[1]

    def edge_rows(rows):
        rows = rows.reshape(PROMPTS * edge_len, rows.shape[2])
        return jnp.pad(rows, ((0, 16 - PROMPTS * edge_len), (0, 0)))

    mixed, kept_states, edge_x_rows, edge_bc_rows = run_mixers(
        member,
        prompt_lengths,
        accepted,
        flat_rows,
        mixer_gain.reshape(1, width),
        w_dt,
        conv_x,
        conv_bc,
        edge_rows(prompt_conv_x),
        edge_rows(prompt_conv_bc),
        jnp.repeat(jnp.stack([dt_bias, ssm_rate, skip_d]), SSM_DIM, axis=1),
        w_query,
        w_kv,
        prompt_kv,
        w_z,
        w_x,
        w_bc,
        prompt_state,
        w_attn_out,
        w_mamba_out,
    )
    edges = edge_x_rows.reshape(row_reqs, draft_len, local_inner)
    kept_bc = edge_bc_rows.reshape(row_reqs, draft_len, 2 * STATE)[:, :edge_len]
    id_grid = draft_ids.reshape(req_count, mdl_count, own_reqs, draft_len)
    column_ids = lax.dynamic_index_in_dim(id_grid, mdl_rank, 1, keepdims=False)
    next_ids = jnp.concatenate([column_ids[..., 1:], column_ids[..., :1]], axis=-1).reshape(1, -1)
    hidden_out, scores_all, kept_all, edges_all = run_tail(
        mixed,
        flat_rows,
        mlp_gain.reshape(1, width),
        final_gain.reshape(1, width),
        jnp.broadcast_to(next_ids, (8, next_ids.shape[1])),
        w_gate,
        w_up,
        w_down,
        head_weight,
        kept_states,
        edges,
    )
    kept_state = kept_all.astype(jnp.float32)
    edge_x = (
        edges_all[:, :, :edge_len]
        .transpose(1, 2, 0, 3)
        .reshape(own_reqs, edge_len, mdl_count * local_inner)
    )
    own_bc = lax.dynamic_slice_in_dim(kept_bc, mdl_rank * own_reqs, own_reqs, 0)
    kept_conv = jnp.concatenate([edge_x, own_bc], axis=2)
    verify_scores = lax.dynamic_slice_in_dim(
        scores_all[0], req_rank * own_tokens, own_tokens, 0
    ).reshape(own_reqs, draft_len)
    return (hidden_out.reshape(own_reqs, draft_len, width), verify_scores, kept_state, kept_conv)


def solution(mesh):
    in_specs = (
        P("req", None, None),
        P(),
        P(None, "mdl"),
        P(),
        P("mdl", None),
        P("req", None, None, None),
        P("req"),
        P("req"),
        P("req"),
        P(None, "mdl"),
        P(None, "mdl"),
        P(),
        P(None, "mdl"),
        P(None, "mdl"),
        P(),
        P("mdl"),
        P("mdl"),
        P("mdl"),
        P("req", "mdl", None, None),
        P("req", None, "mdl"),
        P("req", None, None),
        P("mdl", None),
        P(),
        P(None, "req"),
        P(None, "req"),
        P("req", None),
        P(),
        P("req", None),
        P(),
    )
    out_specs = (
        P(("req", "mdl"), None, None),
        P(("req", "mdl"), None),
        P(("req", "mdl"), None, None, None),
        P(("req", "mdl"), None, None),
    )
    return jax.shard_map(shards, mesh=mesh, in_specs=in_specs, out_specs=out_specs, check_vma=False)
```

```python
import functools

import jax
import jax.numpy as jnp
from jax import lax
from jax.experimental import pallas as pl
from jax.experimental.pallas import tpu as pltpu
from jax.sharding import PartitionSpec as P

Q_HEADS = 8
KV_HEADS = 2
HEAD_DIM = 128
SSM_DIM = 64
STATE = 256
CONV = 4
PROMPTS = 2
P_MAX = 1024
DRAFT = 16
MESH = pl.DeviceIdType.MESH


eps_norm = 1e-05
far_below = -1e30


def rms_scale(values, gain):
    widened = values.astype(jnp.float32)
    spread = jnp.mean(widened * widened, axis=-1, keepdims=True)
    return widened * lax.rsqrt(spread + eps_norm) * gain.astype(jnp.float32)


def dot(a, b):
    return jnp.dot(a, b, preferred_element_type=jnp.float32)


def dot_rows(a, b):
    return lax.dot_general(a, b, (((1,), (1,)), ((), ())), preferred_element_type=jnp.float32)


def dot_exact(a, b):
    return jnp.dot(
        a, b, preferred_element_type=jnp.float32, precision=lax.Precision.HIGHEST
    )


def ones_where(mask, dtype=jnp.bfloat16):
    return jnp.where(mask, 1.0, 0.0).astype(dtype)


def mixer_kernel(
    m,
    member_ref,
    lengths_ref,
    accepted_ref,
    hidden_ref,
    gain_ref,
    w_dt_ref,
    conv_x_ref,
    conv_bc_ref,
    rows_x_ref,
    rows_bc_ref,
    dt_bias_ref,
    rate_ref,
    skip_ref,
    w_query_hbm,
    w_kv_hbm,
    prompt_kv_hbm,
    w_z_hbm,
    w_x_hbm,
    w_bc_hbm,
    state_hbm,
    w_attn_hbm,
    w_mamba_hbm,
    mixed_ref,
    kept_ref,
    edge_x_ref,
    edge_bc_ref,
    w_query,
    w_kv,
    prompt_kv,
    w_z,
    w_x,
    w_bc,
    state,
    w_attn,
    w_mamba,
    normed_ref,
    load_sems,
):
    mdl = lax.axis_index("mdl")
    local_heads = w_query.shape[1] // HEAD_DIM
    group = mdl * local_heads // (Q_HEADS // KV_HEADS)
    pairs = (
        (w_x_hbm, w_x),
        (w_bc_hbm, w_bc),
        (w_z_hbm, w_z),
        (w_query_hbm, w_query),
        (w_kv_hbm.at[group], w_kv),
        (state_hbm, state),
        (prompt_kv_hbm.at[:, group], prompt_kv),
        (w_attn_hbm, w_attn),
        (w_mamba_hbm, w_mamba),
    )
    loads = [
        pltpu.make_async_copy(src, dst, load_sems.at[i]) for i, (src, dst) in enumerate(pairs)
    ]
    for load in loads:
        load.start()

    tokens, width = hidden_ref.shape
    reqs = tokens // DRAFT
    inner = w_x.shape[1]
    heads = inner // SSM_DIM
    edge = CONV - 1
    bf16, f32 = jnp.bfloat16, jnp.float32
    token = lax.broadcasted_iota(jnp.int32, (tokens, 1), 0)
    request, position = token // DRAFT, token % DRAFT
    other = lax.broadcasted_iota(jnp.int32, (1, tokens), 1)
    other_request, other_position = other // DRAFT, other % DRAFT
    member = jnp.zeros((tokens, 1), jnp.int32)
    accepted = jnp.zeros((tokens, 1), jnp.int32)
    for r in range(reqs):
        member = jnp.where(request == r, member_ref[r], member)
        accepted = jnp.where(request == r, accepted_ref[r], accepted)
    first_prompt = member == 0
    valid = jnp.where(first_prompt, lengths_ref[0], lengths_ref[1])
    same = request == other_request
    causal = same & (other_position <= position)

    normed_ref[...] = rms_scale(hidden_ref[...], gain_ref[...]).astype(bf16)
    normed = normed_ref[...]
    dt_in = dot_rows(normed, w_dt_ref[...]).astype(bf16)
    loads[0].wait()
    ssm_in = dot(normed, w_x[...]).astype(bf16)
    loads[1].wait()
    bc_in = dot(normed, w_bc[...]).astype(bf16)

    def starting(rows_ref):
        rows = rows_ref[...].astype(f32)
        return [
            jnp.where(first_prompt, rows[i, 0:1], rows[i, 1:2]) for i in range(edge)
        ]

    keep = position < edge
    kept_at = accepted + position
    pick_drafts = ones_where(same & keep & (other_position == kept_at - edge))

    def kept_rows(series, start):
        kept = dot(pick_drafts, series)
        for i in range(edge):
            kept = jnp.where(keep & (kept_at == i), start[i], kept)
        return kept.astype(bf16)

    start_x, start_bc = starting(rows_x_ref), starting(rows_bc_ref)
    edge_x_ref[...] = kept_rows(ssm_in, start_x)
    edge_bc_ref[...] = kept_rows(bc_in, start_bc)

    def convolved(series, start, taps):
        wide = series.astype(f32)
        total = wide * taps[edge : edge + 1].astype(f32)
        for back in range(1, CONV):
            shifted = pltpu.roll(wide, back, 0)
            for at in range(back):
                shifted = jnp.where(position == at, start[edge + at - back], shifted)
            total = total + shifted * taps[edge - back : edge - back + 1].astype(f32)
        return jax.nn.silu(total)

    x = convolved(ssm_in, start_x, conv_x_ref[...])
    bc = convolved(bc_in, start_bc, conv_bc_ref[...])
    b_part = bc[:, :STATE].astype(bf16)
    c_part = bc[:, STATE:].astype(bf16)

    head_row = lax.broadcasted_iota(jnp.int32, (dt_in.shape[1], inner), 0)
    head_col = lax.broadcasted_iota(jnp.int32, (dt_in.shape[1], inner), 1)
    spread = ones_where(head_row == head_col // SSM_DIM)
    head_at = lax.broadcasted_iota(jnp.int32, (1, inner), 1) // SSM_DIM

    def per_channel(ref):
        values = jnp.zeros((1, inner), f32)
        for h in range(heads):
            values = jnp.where(head_at == h, ref[h], values)
        return values

    dt_bias, rate, skip = per_channel(dt_bias_ref), per_channel(rate_ref), per_channel(skip_ref)
    raw = dot(dt_in, spread) + dt_bias
    step_size = jnp.maximum(raw, 0.0) + jnp.log1p(jnp.exp(-jnp.abs(raw)))
    log_decay = dot_exact(ones_where(causal, f32), -step_size * rate)
    log_rows = log_decay.T
    last = accepted - 1
    final_log = dot_exact(ones_where(same & (other_position == last), f32), log_decay)
    final_rows = jnp.exp(final_log.T)
    carry = jnp.exp(jnp.where(position <= last, final_log - log_decay, far_below)) * step_size
    carried_t = (carry * x).T.astype(bf16)

    loads[5].wait()
    flat = (inner, STATE)
    first_state, second_state = state[0].reshape(flat), state[1].reshape(flat)
    for r in range(reqs):
        own = jnp.where(request == r, b_part, jnp.zeros_like(b_part))
        begin = jnp.where(
            jnp.broadcast_to(member_ref[r], (1, STATE)) == 0, first_state, second_state
        )
        kept = final_rows[:, r * DRAFT : r * DRAFT + 1] * begin + dot(carried_t, own)
        kept_ref[r] = kept.astype(bf16).reshape(heads, SSM_DIM, STATE)

    initial = jnp.where(
        first_prompt,
        dot_rows(c_part, first_state.astype(bf16)),
        dot_rows(c_part, second_state.astype(bf16)),
    )
    overlap = dot_rows(c_part, b_part)
    stepped = (step_size * x).astype(bf16)
    intra = []
    for h in range(heads):
        at = h * SSM_DIM
        gaps = log_decay[:, at : at + 1] - log_rows[at : at + 1, :]
        mixing = jnp.exp(jnp.where(causal, gaps, far_below)) * overlap
        intra.append(dot(mixing.astype(bf16), stepped[:, at : at + SSM_DIM]))
    ssm_out = jnp.concatenate(intra, axis=1) + initial * jnp.exp(log_decay) + skip * x
    loads[2].wait()
    gate_z = dot(normed, w_z[...]).astype(bf16).astype(f32)
    gated = (ssm_out * jax.nn.silu(gate_z)).astype(bf16)

    loads[3].wait()
    queries = dot(normed, w_query[...]).astype(bf16)
    loads[4].wait()
    key_value = dot(normed, w_kv[...]).astype(bf16)
    loads[6].wait()
    scale = HEAD_DIM ** (-0.5)
    usable = lax.broadcasted_iota(jnp.int32, (1, P_MAX), 1) < valid
    attended = []
    for h in range(local_heads):
        query = queries[:, h * HEAD_DIM : (h + 1) * HEAD_DIM]
        scores = jnp.where(
            first_prompt,
            dot_rows(query, prompt_kv[0, :, :HEAD_DIM]),
            dot_rows(query, prompt_kv[1, :, :HEAD_DIM]),
        )
        scores = jnp.where(usable, scores * scale, far_below)
        drafts = jnp.where(causal, dot_rows(query, key_value[:, :HEAD_DIM]) * scale, far_below)
        top = jnp.maximum(
            jnp.max(scores, axis=1, keepdims=True), jnp.max(drafts, axis=1, keepdims=True)
        )
        weights = jnp.exp(scores - top)
        draft_weights = jnp.exp(drafts - top)
        denominator = jnp.sum(weights, axis=1, keepdims=True) + jnp.sum(
            draft_weights, axis=1, keepdims=True
        )
        rounded = weights.astype(bf16)
        summed = jnp.where(
            first_prompt,
            dot(rounded, prompt_kv[0, :, HEAD_DIM:]),
            dot(rounded, prompt_kv[1, :, HEAD_DIM:]),
        ) + dot(draft_weights.astype(bf16), key_value[:, HEAD_DIM:])
        attended.append((summed / denominator).astype(bf16))
    attended = jnp.concatenate(attended, axis=1)
    loads[7].wait()
    loads[8].wait()
    for first in range(0, width, 512):
        at = slice(first, first + 512)
        mixed_ref[:, at] = (dot(attended, w_attn[:, at]) + dot(gated, w_mamba[:, at])).astype(bf16)


def run_mixers(
    member,
    lengths,
    accepted,
    hidden,
    gain,
    w_dt,
    conv_x,
    conv_bc,
    rows_x,
    rows_bc,
    dt_bias,
    ssm_rate,
    skip_d,
    w_query,
    w_kv,
    prompt_kv,
    w_z,
    w_x,
    w_bc,
    state,
    w_attn,
    w_mamba,
):
    m = lax.axis_size("mdl")
    tokens, width = hidden.shape
    reqs = tokens // DRAFT
    smem = pl.BlockSpec(memory_space=pltpu.SMEM)
    vmem = pl.BlockSpec(memory_space=pltpu.VMEM)
    anywhere = pl.BlockSpec(memory_space=pl.ANY)
    bf16 = jnp.bfloat16
    return pl.pallas_call(
        functools.partial(mixer_kernel, m),
        out_shape=(
            jax.ShapeDtypeStruct((tokens, width), bf16),
            jax.ShapeDtypeStruct((reqs,) + state.shape[1:], bf16),
            jax.ShapeDtypeStruct((tokens, w_x.shape[1]), bf16),
            jax.ShapeDtypeStruct((tokens, w_bc.shape[1]), bf16),
        ),
        in_specs=[smem] * 3 + [vmem] * 7 + [smem] * 3 + [anywhere] * 9,
        out_specs=(vmem,) * 4,
        scratch_shapes=[
            pltpu.VMEM(w_query.shape, bf16),
            pltpu.VMEM(w_kv.shape[1:], bf16),
            pltpu.VMEM((PROMPTS,) + prompt_kv.shape[2:], bf16),
            pltpu.VMEM(w_z.shape, bf16),
            pltpu.VMEM(w_x.shape, bf16),
            pltpu.VMEM(w_bc.shape, bf16),
            pltpu.VMEM(state.shape, jnp.float32),
            pltpu.VMEM(w_attn.shape, bf16),
            pltpu.VMEM(w_mamba.shape, bf16),
            pltpu.VMEM((tokens, width), bf16),
            pltpu.SemaphoreType.DMA((9,)),
        ],
        compiler_params=pltpu.CompilerParams(vmem_limit_bytes=63 * 1024 * 1024),
    )(
        member,
        lengths,
        accepted,
        hidden,
        gain,
        w_dt,
        conv_x,
        conv_bc,
        rows_x,
        rows_bc,
        dt_bias,
        ssm_rate,
        skip_d,
        w_query,
        w_kv,
        prompt_kv,
        w_z,
        w_x,
        w_bc,
        state,
        w_attn,
        w_mamba,
    )


def tail_kernel(
    n,
    m,
    mixed_ref,
    hidden_ref,
    mlp_gain_ref,
    final_gain_ref,
    ids_ref,
    gate_hbm,
    up_hbm,
    down_hbm,
    head_hbm,
    kept_hbm,
    edge_ref,
    edge_bc_ref,
    hidden_out_ref,
    verify_ref,
    kept_out,
    kept_conv_ref,
    edge_in,
    gate_w,
    up_w,
    down_w,
    head_w,
    after_ref,
    mix_in,
    rows_ref,
    final_ref,
    final_t,
    active_ref,
    down_ref,
    pair_in,
    chip_send,
    chip_in,
    stats_ref,
    load_sems,
    mix_sems,
    gather_sems,
    final_sems,
    pair_sems,
    chip_sems,
    stats_sems,
    kept_sems,
    edge_sems,
):
    req = lax.axis_index("req")
    mdl = lax.axis_index("mdl")
    chips = n // 2
    chip = req // 2
    core = req % 2
    sibling = chip * 2 + (1 - core)
    block = after_ref.shape[0]
    width = after_ref.shape[1]
    tokens = n * block
    own_reqs = kept_out.shape[0]
    heads = kept_hbm.shape[1]

    loads = [
        pltpu.make_async_copy(src, dst, load_sems.at[i])
        for i, (src, dst) in enumerate(
            ((gate_hbm, gate_w), (up_hbm, up_w), (down_hbm, down_w), (head_hbm, head_w))
        )
    ]
    for load in loads:
        load.start()

    barrier = pltpu.get_barrier_semaphore()
    for d in range(1, m):
        pl.semaphore_signal(
            barrier, inc=1, device_id=(req, (mdl + d) % m), device_id_type=MESH
        )
    for d in range(1, n):
        pl.semaphore_signal(
            barrier, inc=1, device_id=((req + d) % n, mdl), device_id_type=MESH
        )
    pl.semaphore_wait(barrier, m - 1 + n - 1)

    def send(src, dst, sems, index, device):
        copy = pltpu.make_async_remote_copy(
            src_ref=src,
            dst_ref=dst,
            send_sem=sems.at[0, index],
            recv_sem=sems.at[1, index],
            device_id=device,
            device_id_type=MESH,
        )
        copy.start()
        return copy

    mixes = []
    for d in range(1, m):
        to = (mdl + d) % m
        mixes.append(
            send(
                mixed_ref.at[pl.ds(to * block, block)],
                mix_in.at[d - 1],
                mix_sems,
                d - 1,
                (req, to),
            )
        )
    total = mixed_ref[pl.ds(mdl * block, block)].astype(jnp.float32)
    for copy in mixes:
        copy.wait_recv()
    moves = []
    for d in range(1, m):
        to = (mdl + d) % m
        moves.append(
            send(
                kept_hbm.at[pl.ds(to * own_reqs, own_reqs)],
                kept_out.at[:, pl.ds(mdl * heads, heads)],
                kept_sems,
                d - 1,
                (req, to),
            )
        )
        moves.append(
            send(
                edge_ref.at[pl.ds(to * own_reqs, own_reqs)],
                edge_in.at[mdl],
                edge_sems,
                d - 1,
                (req, to),
            )
        )
    own_kept = pltpu.make_async_copy(
        kept_hbm.at[pl.ds(mdl * own_reqs, own_reqs)],
        kept_out.at[:, pl.ds(mdl * heads, heads)],
        load_sems.at[4],
    )
    own_kept.start()
    edge_in[mdl] = edge_ref[pl.ds(mdl * own_reqs, own_reqs)]

    for d in range(m - 1):
        total = total + mix_in[d].astype(jnp.float32)
    after = (
        hidden_ref[pl.ds(mdl * block, block)].astype(jnp.float32) + total
    ).astype(jnp.bfloat16)
    after_ref[...] = after
    rows_ref[req] = rms_scale(after, mlp_gain_ref[...]).astype(jnp.bfloat16)

    def gather_rows(buffer, sems):
        sent = [send(buffer.at[req], buffer.at[req], sems, 0, (sibling, mdl))]
        across = []
        for c in range(1, chips):
            to = (chip + c) % chips * 2 + core
            across.append(send(buffer.at[req], buffer.at[req], sems, c, (to, mdl)))
        for c in range(1, chips):
            across[c - 1].wait_recv()
            source = (chip + chips - c) % chips * 2 + core
            sent.append(
                send(buffer.at[source], buffer.at[source], sems, chips - 1 + c, (sibling, mdl))
            )
        for copy in sent:
            copy.wait_recv()
        return sent + across

    waits = gather_rows(rows_ref, gather_sems)

    for load in loads[:3]:
        load.wait()
    units = gate_w.shape[1]
    unit_step = min(units, 256)
    group = 256 // block
    column_step = 512

    @pl.loop(0, n // group)
    def _(part):
        first = part * group
        prepared = rows_ref[pl.ds(first, group)].reshape(256, width)

        @pl.loop(0, units // unit_step)
        def _(step):
            at = pl.ds(pl.multiple_of(step * unit_step, unit_step), unit_step)
            gate_val = jnp.dot(prepared, gate_w[:, at], preferred_element_type=jnp.float32)
            up_val = jnp.dot(prepared, up_w[:, at], preferred_element_type=jnp.float32)
            active_ref[:, at] = (jax.nn.silu(gate_val) * up_val).astype(jnp.bfloat16)

        @pl.loop(0, width // column_step)
        def _(step):
            at = pl.ds(pl.multiple_of(step * column_step, column_step), column_step)
            value = jnp.dot(active_ref[...], down_w[:, at], preferred_element_type=jnp.float32)
            down_ref[pl.ds(first, group), :, at] = value.astype(jnp.bfloat16).reshape(
                group, block, column_step
            )

    pairs = []
    for c in range(chips):
        to_chip = (chip + 1 + c) % chips
        pairs.append(
            send(
                down_ref.at[to_chip * 2 + (1 - core)],
                pair_in.at[c],
                pair_sems,
                c,
                (sibling, mdl),
            )
        )
    for c in range(chips - 1):
        to = (chip + 1 + c) % chips * 2 + core
        pairs[c].wait_recv()
        chip_send[c] = (
            down_ref[to].astype(jnp.float32) + pair_in[c].astype(jnp.float32)
        ).astype(jnp.bfloat16)
        waits.append(send(chip_send.at[c], chip_in.at[c], chip_sems, c, (to, mdl)))
    pairs[chips - 1].wait_recv()
    summed = down_ref[req].astype(jnp.float32) + pair_in[chips - 1].astype(jnp.float32)
    for c in range(chips - 1):
        waits[-(chips - 1) + c].wait_recv()
        summed = summed + chip_in[c].astype(jnp.float32)
    result = (after_ref[...].astype(jnp.float32) + summed).astype(jnp.bfloat16)
    hidden_out_ref[...] = result
    final_ref[req] = rms_scale(result, final_gain_ref[...]).astype(jnp.bfloat16)
    waits += pairs
    waits += gather_rows(final_ref, final_sems)

    @pl.loop(0, width // 256)
    def _(step):
        at = pl.ds(pl.multiple_of(step * 256, 256), 256)
        final_t[at, :] = (
            final_ref[:, :, at].reshape(tokens, 256).astype(jnp.float32).T.astype(jnp.bfloat16)
        )

    loads[3].wait()
    vocab_here = head_w.shape[0]
    vocab_step = 512
    at_token = lax.broadcasted_iota(jnp.int32, (ids_ref.shape[1], tokens), 1)
    at_request = lax.broadcasted_iota(jnp.int32, (ids_ref.shape[1], tokens), 0)
    own_request = (
        at_token // block * (own_reqs * m) + mdl * own_reqs + at_token % block // DRAFT
    )
    spread = jnp.where(at_request == own_request, 1.0, 0.0)
    by_draft = dot_exact(ids_ref[...].astype(jnp.float32), spread)
    at_draft = lax.broadcasted_iota(jnp.int32, (DRAFT, tokens), 0)
    next_draft = (lax.broadcasted_iota(jnp.int32, (DRAFT, tokens), 1) + 1) % DRAFT
    ids = jnp.sum(
        jnp.where(at_draft == next_draft, by_draft, 0.0), axis=0, keepdims=True
    )
    start = (
        jnp.full((1, tokens), far_below, jnp.float32),
        jnp.zeros((1, tokens), jnp.float32),
        jnp.zeros((1, tokens), jnp.float32),
    )

    def head_step(step, carry):
        top, weight, target = carry
        first = pl.multiple_of(step * vocab_step, vocab_step)
        logits = jnp.dot(
            head_w[pl.ds(first, vocab_step), :], final_t[...], preferred_element_type=jnp.float32
        )
        vocab_ids = (
            req * vocab_here + first + lax.broadcasted_iota(jnp.int32, (vocab_step, tokens), 0)
        )
        target = target + jnp.sum(
            jnp.where(vocab_ids.astype(jnp.float32) == ids, logits, 0.0), axis=0, keepdims=True
        )
        new_top = jnp.maximum(top, jnp.max(logits, axis=0, keepdims=True))
        weight = weight * jnp.exp(top - new_top) + jnp.sum(
            jnp.exp(logits - new_top), axis=0, keepdims=True
        )
        return (new_top, weight, target)

    top, weight, target = lax.fori_loop(0, vocab_here // vocab_step, head_step, start)
    stats_ref[req] = jnp.concatenate(
        [top, weight, target, jnp.zeros((5, tokens), jnp.float32)], axis=0
    )
    shares = [
        send(stats_ref.at[req], stats_ref.at[req], stats_sems, d - 1, ((req + d) % n, mdl))
        for d in range(1, n)
    ]
    for copy in shares:
        copy.wait_recv()
    stats = stats_ref[...]
    tops, weights, targets = stats[:, 0:1, :], stats[:, 1:2, :], stats[:, 2:3, :]
    top = jnp.max(tops, axis=0)
    log_total = top + jnp.log(jnp.sum(weights * jnp.exp(tops - top[None]), axis=0))
    target = jnp.sum(targets, axis=0)
    position = lax.broadcasted_iota(jnp.int32, (1, tokens), 1) % DRAFT
    score = jnp.where(position < DRAFT - 1, target, top) - log_total
    scores = jnp.broadcast_to(score, (8, tokens))
    from_token = lax.broadcasted_iota(jnp.int32, (tokens, DRAFT), 0)
    to_draft = lax.broadcasted_iota(jnp.int32, (tokens, DRAFT), 1)
    verify_ref[...] = jnp.concatenate(
        [
            dot_exact(
                scores,
                jnp.where(from_token == req * block + r * DRAFT + to_draft, 1.0, 0.0),
            )[0:1]
            for r in range(own_reqs)
        ],
        axis=0,
    )

    for copy in mixes + waits + shares:
        copy.wait_send()
    for copy in moves:
        copy.wait()
    own_kept.wait()

    def edge_rows(j, k):
        rows = [edge_in[j, r].astype(jnp.float32)[k : k + 1] for r in range(own_reqs)]
        return jnp.concatenate(rows, axis=0)

    for k in range(CONV - 1):
        bc_rows = [
            edge_bc_ref[mdl * own_reqs + r].astype(jnp.float32)[k : k + 1]
            for r in range(own_reqs)
        ]
        kept_conv_ref[k] = jnp.concatenate(
            [edge_rows(j, k) for j in range(m)] + [jnp.concatenate(bc_rows, axis=0)], axis=1
        ).astype(jnp.bfloat16)


def run_tail(
    mixed, hidden, mlp_gain, final_gain, ids, w_gate, w_up, w_down, head_weight, kept, edges, edges_bc
):
    n = lax.axis_size("req")
    m = lax.axis_size("mdl")
    chips = n // 2
    row_tokens, width = hidden.shape
    block = row_tokens // m
    tokens = n * block
    row_reqs, heads = kept.shape[:2]
    own_reqs = row_reqs // m
    vmem = pl.BlockSpec(memory_space=pltpu.VMEM)
    anywhere = pl.BlockSpec(memory_space=pl.ANY)
    bf16 = jnp.bfloat16
    sems = pltpu.SemaphoreType.DMA
    return pl.pallas_call(
        functools.partial(tail_kernel, n, m),
        out_shape=(
            jax.ShapeDtypeStruct((block, width), bf16),
            jax.ShapeDtypeStruct((own_reqs, DRAFT), jnp.float32),
            jax.ShapeDtypeStruct((own_reqs, heads * m) + kept.shape[2:], bf16),
            jax.ShapeDtypeStruct(
                (CONV - 1, own_reqs, m * edges.shape[2] + edges_bc.shape[2]), bf16
            ),
        ),
        in_specs=[vmem] * 5 + [anywhere] * 5 + [vmem] * 2,
        out_specs=(vmem, vmem, anywhere, vmem),
        scratch_shapes=[
            pltpu.VMEM((m, own_reqs) + edges.shape[1:], bf16),
            pltpu.VMEM(w_gate.shape, bf16),
            pltpu.VMEM(w_up.shape, bf16),
            pltpu.VMEM(w_down.shape, bf16),
            pltpu.VMEM(head_weight.shape, bf16),
            pltpu.VMEM((block, width), bf16),
            pltpu.VMEM((m - 1, block, width), bf16),
            pltpu.VMEM((n, block, width), bf16),
            pltpu.VMEM((n, block, width), bf16),
            pltpu.VMEM((width, tokens), bf16),
            pltpu.VMEM((256, w_gate.shape[1]), bf16),
            pltpu.VMEM((n, block, width), bf16),
            pltpu.VMEM((chips, block, width), bf16),
            pltpu.VMEM((chips - 1, block, width), bf16),
            pltpu.VMEM((chips - 1, block, width), bf16),
            pltpu.VMEM((n, 8, tokens), jnp.float32),
            sems((5,)),
            sems((2, m - 1)),
            sems((2, 2 * chips - 1)),
            sems((2, 2 * chips - 1)),
            sems((2, chips)),
            sems((2, chips - 1)),
            sems((2, n - 1)),
            sems((2, m - 1)),
            sems((2, m - 1)),
        ],
        compiler_params=pltpu.CompilerParams(
            collective_id=0, has_side_effects=True, vmem_limit_bytes=63 * 1024 * 1024
        ),
    )(
        mixed, hidden, mlp_gain, final_gain, ids, w_gate, w_up, w_down, head_weight, kept, edges, edges_bc
    )


def shards(
    hidden_in,
    mixer_gain,
    w_query,
    w_kv,
    w_attn_out,
    prompt_kv,
    prompt_lengths,
    member,
    accepted,
    w_z,
    w_x,
    w_bc,
    w_dt,
    conv_x,
    conv_bc,
    ssm_rate,
    dt_bias,
    skip_d,
    prompt_state,
    prompt_conv_x,
    prompt_conv_bc,
    w_mamba_out,
    mlp_gain,
    w_gate,
    w_up,
    w_down,
    final_gain,
    head_weight,
    draft_ids,
):
    row_reqs, draft_len, width = hidden_in.shape
    own_reqs = row_reqs // lax.axis_size("mdl")
    local_inner = w_x.shape[1]
    flat_rows = hidden_in.reshape(row_reqs * draft_len, width)
    mixed, kept_states, edge_x_rows, edge_bc_rows = run_mixers(
        member,
        prompt_lengths,
        accepted,
        flat_rows,
        mixer_gain,
        w_dt.T,
        conv_x,
        conv_bc,
        prompt_conv_x.transpose(1, 0, 2),
        prompt_conv_bc.transpose(1, 0, 2),
        dt_bias,
        ssm_rate,
        skip_d,
        w_query,
        w_kv,
        prompt_kv,
        w_z,
        w_x,
        w_bc,
        prompt_state,
        w_attn_out,
        w_mamba_out,
    )
    hidden_out, verify_scores, kept_all, kept_conv = run_tail(
        mixed,
        flat_rows,
        mlp_gain,
        final_gain,
        draft_ids.T,
        w_gate,
        w_up,
        w_down,
        head_weight,
        kept_states,
        edge_x_rows.reshape(row_reqs, draft_len, local_inner),
        edge_bc_rows.reshape(row_reqs, draft_len, 2 * STATE),
    )
    return (
        hidden_out.reshape(own_reqs, draft_len, width),
        verify_scores,
        kept_all.astype(jnp.float32),
        kept_conv.transpose(1, 0, 2),
    )


def solution(mesh):
    in_specs = (
        P("req", None, None),
        P(),
        P(None, "mdl"),
        P(),
        P("mdl", None),
        P("req", None, None, None),
        P("req"),
        P("req"),
        P("req"),
        P(None, "mdl"),
        P(None, "mdl"),
        P(),
        P(None, "mdl"),
        P(None, "mdl"),
        P(),
        P("mdl"),
        P("mdl"),
        P("mdl"),
        P("req", "mdl", None, None),
        P("req", None, "mdl"),
        P("req", None, None),
        P("mdl", None),
        P(),
        P(None, "req"),
        P(None, "req"),
        P("req", None),
        P(),
        P("req", None),
        P(),
    )
    out_specs = (
        P(("req", "mdl"), None, None),
        P(("req", "mdl"), None),
        P(("req", "mdl"), None, None, None),
        P(("req", "mdl"), None, None),
    )
    return jax.shard_map(shards, mesh=mesh, in_specs=in_specs, out_specs=out_specs, check_vma=False)
```

```python
import functools

import jax
import jax.numpy as jnp
from jax import lax
from jax.experimental import pallas as pl
from jax.experimental.pallas import tpu as pltpu
from jax.sharding import PartitionSpec as P

Q_HEADS = 8
KV_HEADS = 2
HEAD_DIM = 128
SSM_DIM = 64
STATE = 256
CONV = 4
PROMPTS = 2
P_MAX = 1024
DRAFT = 16
MESH = pl.DeviceIdType.MESH


eps_norm = 1e-05
far_below = -1e30


def rms_scale(values, gain):
    widened = values.astype(jnp.float32)
    spread = jnp.mean(widened * widened, axis=-1, keepdims=True)
    return widened * lax.rsqrt(spread + eps_norm) * gain.astype(jnp.float32)


def dot(a, b):
    return jnp.dot(a, b, preferred_element_type=jnp.float32)


def dot_rows(a, b):
    return lax.dot_general(a, b, (((1,), (1,)), ((), ())), preferred_element_type=jnp.float32)


def dot_exact(a, b):
    return jnp.dot(
        a, b, preferred_element_type=jnp.float32, precision=lax.Precision.HIGHEST
    )


def ones_where(mask, dtype=jnp.bfloat16):
    return jnp.where(mask, 1.0, 0.0).astype(dtype)


def mixer_kernel(
    m,
    member_ref,
    lengths_ref,
    accepted_ref,
    hidden_ref,
    gain_ref,
    w_dt_ref,
    conv_x_ref,
    conv_bc_ref,
    rows_x_ref,
    rows_bc_ref,
    dt_bias_ref,
    rate_ref,
    skip_ref,
    w_query_hbm,
    w_kv_hbm,
    prompt_kv_hbm,
    w_z_hbm,
    w_x_hbm,
    w_bc_hbm,
    state_hbm,
    w_attn_hbm,
    w_mamba_hbm,
    mixed_ref,
    kept_ref,
    edge_x_ref,
    edge_bc_ref,
    w_query,
    w_kv,
    prompt_kv,
    w_z,
    w_x,
    w_bc,
    state,
    w_attn,
    w_mamba,
    normed_ref,
    load_sems,
):
    mdl = lax.axis_index("mdl")
    local_heads = w_query.shape[1] // HEAD_DIM
    group = mdl * local_heads // (Q_HEADS // KV_HEADS)
    pairs = (
        (w_x_hbm, w_x),
        (w_bc_hbm, w_bc),
        (w_z_hbm, w_z),
        (w_query_hbm, w_query),
        (w_kv_hbm.at[group], w_kv),
        (state_hbm, state),
        (prompt_kv_hbm.at[:, group], prompt_kv),
        (w_attn_hbm, w_attn),
        (w_mamba_hbm, w_mamba),
    )
    loads = [
        pltpu.make_async_copy(src, dst, load_sems.at[i]) for i, (src, dst) in enumerate(pairs)
    ]
    for load in loads:
        load.start()

    tokens, width = hidden_ref.shape
    reqs = tokens // DRAFT
    inner = w_x.shape[1]
    heads = inner // SSM_DIM
    edge = CONV - 1
    bf16, f32 = jnp.bfloat16, jnp.float32
    token = lax.broadcasted_iota(jnp.int32, (tokens, 1), 0)
    request, position = token // DRAFT, token % DRAFT
    other = lax.broadcasted_iota(jnp.int32, (1, tokens), 1)
    other_request, other_position = other // DRAFT, other % DRAFT
    member = jnp.zeros((tokens, 1), jnp.int32)
    accepted = jnp.zeros((tokens, 1), jnp.int32)
    for r in range(reqs):
        member = jnp.where(request == r, member_ref[r], member)
        accepted = jnp.where(request == r, accepted_ref[r], accepted)
    first_prompt = member == 0
    valid = jnp.where(first_prompt, lengths_ref[0], lengths_ref[1])
    same = request == other_request
    causal = same & (other_position <= position)

    normed_ref[...] = rms_scale(hidden_ref[...], gain_ref[...]).astype(bf16)
    normed = normed_ref[...]
    dt_in = dot_rows(normed, w_dt_ref[...]).astype(bf16)
    loads[0].wait()
    ssm_in = dot(normed, w_x[...]).astype(bf16)
    loads[1].wait()
    bc_in = dot(normed, w_bc[...]).astype(bf16)

    def starting(rows_ref):
        rows = rows_ref[...].astype(f32)
        return [
            jnp.where(first_prompt, rows[i, 0:1], rows[i, 1:2]) for i in range(edge)
        ]

    keep = position < edge
    kept_at = accepted + position
    pick_drafts = ones_where(same & keep & (other_position == kept_at - edge))

    def kept_rows(series, start):
        kept = dot(pick_drafts, series)
        for i in range(edge):
            kept = jnp.where(keep & (kept_at == i), start[i], kept)
        return kept.astype(bf16)

    start_x, start_bc = starting(rows_x_ref), starting(rows_bc_ref)
    edge_x_ref[...] = kept_rows(ssm_in, start_x)
    edge_bc_ref[...] = kept_rows(bc_in, start_bc)

    def convolved(series, start, taps):
        wide = series.astype(f32)
        total = wide * taps[edge : edge + 1].astype(f32)
        for back in range(1, CONV):
            shifted = pltpu.roll(wide, back, 0)
            for at in range(back):
                shifted = jnp.where(position == at, start[edge + at - back], shifted)
            total = total + shifted * taps[edge - back : edge - back + 1].astype(f32)
        return jax.nn.silu(total)

    x = convolved(ssm_in, start_x, conv_x_ref[...])
    bc = convolved(bc_in, start_bc, conv_bc_ref[...])
    b_part = bc[:, :STATE].astype(bf16)
    c_part = bc[:, STATE:].astype(bf16)

    head_row = lax.broadcasted_iota(jnp.int32, (dt_in.shape[1], inner), 0)
    head_col = lax.broadcasted_iota(jnp.int32, (dt_in.shape[1], inner), 1)
    spread = ones_where(head_row == head_col // SSM_DIM)
    head_at = lax.broadcasted_iota(jnp.int32, (1, inner), 1) // SSM_DIM

    def per_channel(ref):
        values = jnp.zeros((1, inner), f32)
        for h in range(heads):
            values = jnp.where(head_at == h, ref[h], values)
        return values

    dt_bias, rate, skip = per_channel(dt_bias_ref), per_channel(rate_ref), per_channel(skip_ref)
    raw = dot(dt_in, spread) + dt_bias
    step_size = jnp.maximum(raw, 0.0) + jnp.log1p(jnp.exp(-jnp.abs(raw)))
    log_decay = dot_exact(ones_where(causal, f32), -step_size * rate)
    log_rows = log_decay.T
    last = accepted - 1
    final_log = dot_exact(ones_where(same & (other_position == last), f32), log_decay)
    final_rows = jnp.exp(final_log.T)
    carry = jnp.exp(jnp.where(position <= last, final_log - log_decay, far_below)) * step_size
    carried_t = (carry * x).T.astype(bf16)

    loads[5].wait()
    flat = (inner, STATE)
    first_state, second_state = state[0].reshape(flat), state[1].reshape(flat)
    for r in range(reqs):
        own = jnp.where(request == r, b_part, jnp.zeros_like(b_part))
        begin = jnp.where(
            jnp.broadcast_to(member_ref[r], (1, STATE)) == 0, first_state, second_state
        )
        kept = final_rows[:, r * DRAFT : r * DRAFT + 1] * begin + dot(carried_t, own)
        kept_ref[r] = kept.astype(bf16).reshape(heads, SSM_DIM, STATE)

    initial = jnp.where(
        first_prompt,
        dot_rows(c_part, first_state.astype(bf16)),
        dot_rows(c_part, second_state.astype(bf16)),
    )
    overlap = dot_rows(c_part, b_part)
    stepped = (step_size * x).astype(bf16)
    intra = []
    for h in range(heads):
        at = h * SSM_DIM
        gaps = log_decay[:, at : at + 1] - log_rows[at : at + 1, :]
        mixing = jnp.exp(jnp.where(causal, gaps, far_below)) * overlap
        intra.append(dot(mixing.astype(bf16), stepped[:, at : at + SSM_DIM]))
    ssm_out = jnp.concatenate(intra, axis=1) + initial * jnp.exp(log_decay) + skip * x
    loads[2].wait()
    gate_z = dot(normed, w_z[...]).astype(bf16).astype(f32)
    gated = (ssm_out * jax.nn.silu(gate_z)).astype(bf16)

    loads[3].wait()
    queries = dot(normed, w_query[...]).astype(bf16)
    loads[4].wait()
    key_value = dot(normed, w_kv[...]).astype(bf16)
    loads[6].wait()
    scale = HEAD_DIM ** (-0.5)
    usable = lax.broadcasted_iota(jnp.int32, (1, P_MAX), 1) < valid
    attended = []
    for h in range(local_heads):
        query = queries[:, h * HEAD_DIM : (h + 1) * HEAD_DIM]
        scores = jnp.where(
            first_prompt,
            dot_rows(query, prompt_kv[0, :, :HEAD_DIM]),
            dot_rows(query, prompt_kv[1, :, :HEAD_DIM]),
        )
        scores = jnp.where(usable, scores * scale, far_below)
        drafts = jnp.where(causal, dot_rows(query, key_value[:, :HEAD_DIM]) * scale, far_below)
        top = jnp.maximum(
            jnp.max(scores, axis=1, keepdims=True), jnp.max(drafts, axis=1, keepdims=True)
        )
        weights = jnp.exp(scores - top)
        draft_weights = jnp.exp(drafts - top)
        denominator = jnp.sum(weights, axis=1, keepdims=True) + jnp.sum(
            draft_weights, axis=1, keepdims=True
        )
        rounded = weights.astype(bf16)
        summed = jnp.where(
            first_prompt,
            dot(rounded, prompt_kv[0, :, HEAD_DIM:]),
            dot(rounded, prompt_kv[1, :, HEAD_DIM:]),
        ) + dot(draft_weights.astype(bf16), key_value[:, HEAD_DIM:])
        attended.append((summed / denominator).astype(bf16))
    attended = jnp.concatenate(attended, axis=1)
    loads[7].wait()
    loads[8].wait()
    for first in range(0, width, 512):
        at = slice(first, first + 512)
        mixed_ref[:, at] = (dot(attended, w_attn[:, at]) + dot(gated, w_mamba[:, at])).astype(bf16)


def run_mixers(
    member,
    lengths,
    accepted,
    hidden,
    gain,
    w_dt,
    conv_x,
    conv_bc,
    rows_x,
    rows_bc,
    dt_bias,
    ssm_rate,
    skip_d,
    w_query,
    w_kv,
    prompt_kv,
    w_z,
    w_x,
    w_bc,
    state,
    w_attn,
    w_mamba,
):
    m = lax.axis_size("mdl")
    tokens, width = hidden.shape
    reqs = tokens // DRAFT
    smem = pl.BlockSpec(memory_space=pltpu.SMEM)
    vmem = pl.BlockSpec(memory_space=pltpu.VMEM)
    anywhere = pl.BlockSpec(memory_space=pl.ANY)
    bf16 = jnp.bfloat16
    return pl.pallas_call(
        functools.partial(mixer_kernel, m),
        out_shape=(
            jax.ShapeDtypeStruct((tokens, width), bf16),
            jax.ShapeDtypeStruct((reqs,) + state.shape[1:], bf16),
            jax.ShapeDtypeStruct((tokens, w_x.shape[1]), bf16),
            jax.ShapeDtypeStruct((tokens, w_bc.shape[1]), bf16),
        ),
        in_specs=[smem] * 3 + [vmem] * 7 + [smem] * 3 + [anywhere] * 9,
        out_specs=(vmem,) * 4,
        scratch_shapes=[
            pltpu.VMEM(w_query.shape, bf16),
            pltpu.VMEM(w_kv.shape[1:], bf16),
            pltpu.VMEM((PROMPTS,) + prompt_kv.shape[2:], bf16),
            pltpu.VMEM(w_z.shape, bf16),
            pltpu.VMEM(w_x.shape, bf16),
            pltpu.VMEM(w_bc.shape, bf16),
            pltpu.VMEM(state.shape, jnp.float32),
            pltpu.VMEM(w_attn.shape, bf16),
            pltpu.VMEM(w_mamba.shape, bf16),
            pltpu.VMEM((tokens, width), bf16),
            pltpu.SemaphoreType.DMA((9,)),
        ],
        compiler_params=pltpu.CompilerParams(vmem_limit_bytes=63 * 1024 * 1024),
    )(
        member,
        lengths,
        accepted,
        hidden,
        gain,
        w_dt,
        conv_x,
        conv_bc,
        rows_x,
        rows_bc,
        dt_bias,
        ssm_rate,
        skip_d,
        w_query,
        w_kv,
        prompt_kv,
        w_z,
        w_x,
        w_bc,
        state,
        w_attn,
        w_mamba,
    )


def tail_kernel(
    n,
    m,
    mixed_ref,
    hidden_ref,
    mlp_gain_ref,
    final_gain_ref,
    ids_ref,
    gate_hbm,
    up_hbm,
    down_hbm,
    head_hbm,
    kept_hbm,
    edge_ref,
    edge_bc_ref,
    hidden_out_ref,
    verify_ref,
    kept_out,
    kept_conv_ref,
    edge_in,
    gate_w,
    up_w,
    down_w,
    head_w,
    after_ref,
    mix_in,
    rows_ref,
    final_ref,
    final_t,
    active_ref,
    down_ref,
    pair_in,
    chip_send,
    chip_in,
    stats_ref,
    load_sems,
    mix_sems,
    gather_sems,
    final_sems,
    pair_sems,
    chip_sems,
    stats_sems,
    kept_sems,
    edge_sems,
):
    req = lax.axis_index("req")
    mdl = lax.axis_index("mdl")
    chips = n // 2
    chip = req // 2
    core = req % 2
    sibling = chip * 2 + (1 - core)
    block = after_ref.shape[0]
    width = after_ref.shape[1]
    tokens = n * block
    own_reqs = kept_out.shape[0]
    heads = kept_hbm.shape[1]

    loads = [
        pltpu.make_async_copy(src, dst, load_sems.at[i])
        for i, (src, dst) in enumerate(
            ((gate_hbm, gate_w), (up_hbm, up_w), (down_hbm, down_w), (head_hbm, head_w))
        )
    ]
    for load in loads:
        load.start()

    barrier = pltpu.get_barrier_semaphore()
    for d in range(1, m):
        pl.semaphore_signal(
            barrier, inc=1, device_id=(req, (mdl + d) % m), device_id_type=MESH
        )
    for d in range(1, n):
        pl.semaphore_signal(
            barrier, inc=1, device_id=((req + d) % n, mdl), device_id_type=MESH
        )
    pl.semaphore_wait(barrier, m - 1 + n - 1)

    def send(src, dst, sems, index, device):
        copy = pltpu.make_async_remote_copy(
            src_ref=src,
            dst_ref=dst,
            send_sem=sems.at[0, index],
            recv_sem=sems.at[1, index],
            device_id=device,
            device_id_type=MESH,
        )
        copy.start()
        return copy

    mixes = []
    for d in range(1, m):
        to = (mdl + d) % m
        mixes.append(
            send(
                mixed_ref.at[pl.ds(to * block, block)],
                mix_in.at[d - 1],
                mix_sems,
                d - 1,
                (req, to),
            )
        )
    total = mixed_ref[pl.ds(mdl * block, block)].astype(jnp.float32)
    for copy in mixes:
        copy.wait_recv()
    moves = []
    for d in range(1, m):
        to = (mdl + d) % m
        moves.append(
            send(
                kept_hbm.at[pl.ds(to * own_reqs, own_reqs)],
                kept_out.at[:, pl.ds(mdl * heads, heads)],
                kept_sems,
                d - 1,
                (req, to),
            )
        )
        moves.append(
            send(
                edge_ref.at[pl.ds(to * own_reqs, own_reqs)],
                edge_in.at[mdl],
                edge_sems,
                d - 1,
                (req, to),
            )
        )
    own_kept = pltpu.make_async_copy(
        kept_hbm.at[pl.ds(mdl * own_reqs, own_reqs)],
        kept_out.at[:, pl.ds(mdl * heads, heads)],
        load_sems.at[4],
    )
    own_kept.start()
    edge_in[mdl] = edge_ref[pl.ds(mdl * own_reqs, own_reqs)]

    for d in range(m - 1):
        total = total + mix_in[d].astype(jnp.float32)
    after = (
        hidden_ref[pl.ds(mdl * block, block)].astype(jnp.float32) + total
    ).astype(jnp.bfloat16)
    after_ref[...] = after
    rows_ref[req] = rms_scale(after, mlp_gain_ref[...]).astype(jnp.bfloat16)

    def gather_rows(buffer, sems):
        sent = [send(buffer.at[req], buffer.at[req], sems, 0, (sibling, mdl))]
        across = []
        for c in range(1, chips):
            to = (chip + c) % chips * 2 + core
            across.append(send(buffer.at[req], buffer.at[req], sems, c, (to, mdl)))
        for c in range(1, chips):
            across[c - 1].wait_recv()
            source = (chip + chips - c) % chips * 2 + core
            sent.append(
                send(buffer.at[source], buffer.at[source], sems, chips - 1 + c, (sibling, mdl))
            )
        for copy in sent:
            copy.wait_recv()
        return sent + across

    waits = gather_rows(rows_ref, gather_sems)

    for load in loads[:3]:
        load.wait()
    units = gate_w.shape[1]
    unit_step = min(units, 256)
    group = 256 // block
    column_step = 512

    @pl.loop(0, n // group)
    def _(part):
        first = part * group
        prepared = rows_ref[pl.ds(first, group)].reshape(256, width)

        @pl.loop(0, units // unit_step, unroll=units // unit_step)
        def _(step):
            at = pl.ds(pl.multiple_of(step * unit_step, unit_step), unit_step)
            gate_val = jnp.dot(prepared, gate_w[:, at], preferred_element_type=jnp.float32)
            up_val = jnp.dot(prepared, up_w[:, at], preferred_element_type=jnp.float32)
            active_ref[:, at] = (jax.nn.silu(gate_val) * up_val).astype(jnp.bfloat16)

        @pl.loop(0, width // column_step, unroll=2)
        def _(step):
            at = pl.ds(pl.multiple_of(step * column_step, column_step), column_step)
            value = jnp.dot(active_ref[...], down_w[:, at], preferred_element_type=jnp.float32)
            down_ref[pl.ds(first, group), :, at] = value.astype(jnp.bfloat16).reshape(
                group, block, column_step
            )

    pairs = []
    for c in range(chips):
        to_chip = (chip + 1 + c) % chips
        pairs.append(
            send(
                down_ref.at[to_chip * 2 + (1 - core)],
                pair_in.at[c],
                pair_sems,
                c,
                (sibling, mdl),
            )
        )
    for c in range(chips - 1):
        to = (chip + 1 + c) % chips * 2 + core
        pairs[c].wait_recv()
        chip_send[c] = (
            down_ref[to].astype(jnp.float32) + pair_in[c].astype(jnp.float32)
        ).astype(jnp.bfloat16)
        waits.append(send(chip_send.at[c], chip_in.at[c], chip_sems, c, (to, mdl)))
    pairs[chips - 1].wait_recv()
    summed = down_ref[req].astype(jnp.float32) + pair_in[chips - 1].astype(jnp.float32)
    for c in range(chips - 1):
        waits[-(chips - 1) + c].wait_recv()
        summed = summed + chip_in[c].astype(jnp.float32)
    result = (after_ref[...].astype(jnp.float32) + summed).astype(jnp.bfloat16)
    hidden_out_ref[...] = result
    final_ref[req] = rms_scale(result, final_gain_ref[...]).astype(jnp.bfloat16)
    waits += pairs
    waits += gather_rows(final_ref, final_sems)

    @pl.loop(0, width // 256, unroll=4)
    def _(step):
        at = pl.ds(pl.multiple_of(step * 256, 256), 256)
        final_t[at, :] = (
            final_ref[:, :, at].reshape(tokens, 256).astype(jnp.float32).T.astype(jnp.bfloat16)
        )

    loads[3].wait()
    vocab_here = head_w.shape[0]
    vocab_step = 512
    at_token = lax.broadcasted_iota(jnp.int32, (ids_ref.shape[1], tokens), 1)
    at_request = lax.broadcasted_iota(jnp.int32, (ids_ref.shape[1], tokens), 0)
    own_request = (
        at_token // block * (own_reqs * m) + mdl * own_reqs + at_token % block // DRAFT
    )
    spread = jnp.where(at_request == own_request, 1.0, 0.0)
    by_draft = dot_exact(ids_ref[...].astype(jnp.float32), spread)
    at_draft = lax.broadcasted_iota(jnp.int32, (DRAFT, tokens), 0)
    next_draft = (lax.broadcasted_iota(jnp.int32, (DRAFT, tokens), 1) + 1) % DRAFT
    ids = jnp.sum(
        jnp.where(at_draft == next_draft, by_draft, 0.0), axis=0, keepdims=True
    )
    start = (
        jnp.full((1, tokens), far_below, jnp.float32),
        jnp.zeros((1, tokens), jnp.float32),
        jnp.zeros((1, tokens), jnp.float32),
    )

    def head_step(step, carry):
        top, weight, target = carry
        first = pl.multiple_of(step * vocab_step, vocab_step)
        logits = jnp.dot(
            head_w[pl.ds(first, vocab_step), :], final_t[...], preferred_element_type=jnp.float32
        )
        vocab_ids = (
            req * vocab_here + first + lax.broadcasted_iota(jnp.int32, (vocab_step, tokens), 0)
        )
        target = target + jnp.sum(
            jnp.where(vocab_ids.astype(jnp.float32) == ids, logits, 0.0), axis=0, keepdims=True
        )
        new_top = jnp.maximum(top, jnp.max(logits, axis=0, keepdims=True))
        weight = weight * jnp.exp(top - new_top) + jnp.sum(
            jnp.exp(logits - new_top), axis=0, keepdims=True
        )
        return (new_top, weight, target)

    top, weight, target = lax.fori_loop(
        0, vocab_here // vocab_step, head_step, start, unroll=min(4, vocab_here // vocab_step)
    )
    stats_ref[req] = jnp.concatenate(
        [top, weight, target, jnp.zeros((5, tokens), jnp.float32)], axis=0
    )
    shares = [
        send(stats_ref.at[req], stats_ref.at[req], stats_sems, d - 1, ((req + d) % n, mdl))
        for d in range(1, n)
    ]
    for copy in shares:
        copy.wait_recv()
    stats = stats_ref[...]
    tops, weights, targets = stats[:, 0:1, :], stats[:, 1:2, :], stats[:, 2:3, :]
    top = jnp.max(tops, axis=0)
    log_total = top + jnp.log(jnp.sum(weights * jnp.exp(tops - top[None]), axis=0))
    target = jnp.sum(targets, axis=0)
    position = lax.broadcasted_iota(jnp.int32, (1, tokens), 1) % DRAFT
    score = jnp.where(position < DRAFT - 1, target, top) - log_total
    scores = jnp.broadcast_to(score, (8, tokens))
    from_token = lax.broadcasted_iota(jnp.int32, (tokens, DRAFT), 0)
    to_draft = lax.broadcasted_iota(jnp.int32, (tokens, DRAFT), 1)
    verify_ref[...] = jnp.concatenate(
        [
            dot_exact(
                scores,
                jnp.where(from_token == req * block + r * DRAFT + to_draft, 1.0, 0.0),
            )[0:1]
            for r in range(own_reqs)
        ],
        axis=0,
    )

    for copy in mixes + waits + shares:
        copy.wait_send()
    for copy in moves:
        copy.wait()
    own_kept.wait()

    def edge_rows(j, k):
        rows = [edge_in[j, r].astype(jnp.float32)[k : k + 1] for r in range(own_reqs)]
        return jnp.concatenate(rows, axis=0)

    for k in range(CONV - 1):
        bc_rows = [
            edge_bc_ref[mdl * own_reqs + r].astype(jnp.float32)[k : k + 1]
            for r in range(own_reqs)
        ]
        kept_conv_ref[k] = jnp.concatenate(
            [edge_rows(j, k) for j in range(m)] + [jnp.concatenate(bc_rows, axis=0)], axis=1
        ).astype(jnp.bfloat16)


def run_tail(
    mixed, hidden, mlp_gain, final_gain, ids, w_gate, w_up, w_down, head_weight, kept, edges, edges_bc
):
    n = lax.axis_size("req")
    m = lax.axis_size("mdl")
    chips = n // 2
    row_tokens, width = hidden.shape
    block = row_tokens // m
    tokens = n * block
    row_reqs, heads = kept.shape[:2]
    own_reqs = row_reqs // m
    vmem = pl.BlockSpec(memory_space=pltpu.VMEM)
    anywhere = pl.BlockSpec(memory_space=pl.ANY)
    bf16 = jnp.bfloat16
    sems = pltpu.SemaphoreType.DMA
    return pl.pallas_call(
        functools.partial(tail_kernel, n, m),
        out_shape=(
            jax.ShapeDtypeStruct((block, width), bf16),
            jax.ShapeDtypeStruct((own_reqs, DRAFT), jnp.float32),
            jax.ShapeDtypeStruct((own_reqs, heads * m) + kept.shape[2:], bf16),
            jax.ShapeDtypeStruct(
                (CONV - 1, own_reqs, m * edges.shape[2] + edges_bc.shape[2]), bf16
            ),
        ),
        in_specs=[vmem] * 5 + [anywhere] * 5 + [vmem] * 2,
        out_specs=(vmem, vmem, anywhere, vmem),
        scratch_shapes=[
            pltpu.VMEM((m, own_reqs) + edges.shape[1:], bf16),
            pltpu.VMEM(w_gate.shape, bf16),
            pltpu.VMEM(w_up.shape, bf16),
            pltpu.VMEM(w_down.shape, bf16),
            pltpu.VMEM(head_weight.shape, bf16),
            pltpu.VMEM((block, width), bf16),
            pltpu.VMEM((m - 1, block, width), bf16),
            pltpu.VMEM((n, block, width), bf16),
            pltpu.VMEM((n, block, width), bf16),
            pltpu.VMEM((width, tokens), bf16),
            pltpu.VMEM((256, w_gate.shape[1]), bf16),
            pltpu.VMEM((n, block, width), bf16),
            pltpu.VMEM((chips, block, width), bf16),
            pltpu.VMEM((chips - 1, block, width), bf16),
            pltpu.VMEM((chips - 1, block, width), bf16),
            pltpu.VMEM((n, 8, tokens), jnp.float32),
            sems((5,)),
            sems((2, m - 1)),
            sems((2, 2 * chips - 1)),
            sems((2, 2 * chips - 1)),
            sems((2, chips)),
            sems((2, chips - 1)),
            sems((2, n - 1)),
            sems((2, m - 1)),
            sems((2, m - 1)),
        ],
        compiler_params=pltpu.CompilerParams(
            collective_id=0, has_side_effects=True, vmem_limit_bytes=63 * 1024 * 1024
        ),
    )(
        mixed, hidden, mlp_gain, final_gain, ids, w_gate, w_up, w_down, head_weight, kept, edges, edges_bc
    )


def shards(
    hidden_in,
    mixer_gain,
    w_query,
    w_kv,
    w_attn_out,
    prompt_kv,
    prompt_lengths,
    member,
    accepted,
    w_z,
    w_x,
    w_bc,
    w_dt,
    conv_x,
    conv_bc,
    ssm_rate,
    dt_bias,
    skip_d,
    prompt_state,
    prompt_conv_x,
    prompt_conv_bc,
    w_mamba_out,
    mlp_gain,
    w_gate,
    w_up,
    w_down,
    final_gain,
    head_weight,
    draft_ids,
):
    row_reqs, draft_len, width = hidden_in.shape
    own_reqs = row_reqs // lax.axis_size("mdl")
    local_inner = w_x.shape[1]
    flat_rows = hidden_in.reshape(row_reqs * draft_len, width)
    mixed, kept_states, edge_x_rows, edge_bc_rows = run_mixers(
        member,
        prompt_lengths,
        accepted,
        flat_rows,
        mixer_gain,
        w_dt.T,
        conv_x,
        conv_bc,
        prompt_conv_x.transpose(1, 0, 2),
        prompt_conv_bc.transpose(1, 0, 2),
        dt_bias,
        ssm_rate,
        skip_d,
        w_query,
        w_kv,
        prompt_kv,
        w_z,
        w_x,
        w_bc,
        prompt_state,
        w_attn_out,
        w_mamba_out,
    )
    hidden_out, verify_scores, kept_all, kept_conv = run_tail(
        mixed,
        flat_rows,
        mlp_gain,
        final_gain,
        draft_ids.T,
        w_gate,
        w_up,
        w_down,
        head_weight,
        kept_states,
        edge_x_rows.reshape(row_reqs, draft_len, local_inner),
        edge_bc_rows.reshape(row_reqs, draft_len, 2 * STATE),
    )
    return (
        hidden_out.reshape(own_reqs, draft_len, width),
        verify_scores,
        kept_all.astype(jnp.float32),
        kept_conv.transpose(1, 0, 2),
    )


def solution(mesh):
    in_specs = (
        P("req", None, None),
        P(),
        P(None, "mdl"),
        P(),
        P("mdl", None),
        P("req", None, None, None),
        P("req"),
        P("req"),
        P("req"),
        P(None, "mdl"),
        P(None, "mdl"),
        P(),
        P(None, "mdl"),
        P(None, "mdl"),
        P(),
        P("mdl"),
        P("mdl"),
        P("mdl"),
        P("req", "mdl", None, None),
        P("req", None, "mdl"),
        P("req", None, None),
        P("mdl", None),
        P(),
        P(None, "req"),
        P(None, "req"),
        P("req", None),
        P(),
        P("req", None),
        P(),
    )
    out_specs = (
        P(("req", "mdl"), None, None),
        P(("req", "mdl"), None),
        P(("req", "mdl"), None, None, None),
        P(("req", "mdl"), None, None),
    )
    return jax.shard_map(shards, mesh=mesh, in_specs=in_specs, out_specs=out_specs, check_vma=False)
```
